32 devices in a mesh: member: 2 (over y), lat: 4 (over z), lon: 2 (over x), lev: 2 (over core).
Axes of the slice: x: 2, y: 2, z: 4, core: 2. Of those that a mesh axis runs over, the one named last changes fastest.
Arguments:
- adjoint_in: float32 [10, 16, 32, 1152], P('member', 'lev', 'lat', 'lon'), parts along dimension 0, may hold values from -12 to 12
- lat_ahead: float32 [32, 32, 1152], P(('member', 'lev'), 'lat', 'lon'), parts along dimension 0, may hold values from 0.35 to 0.8
- lat_behind: float32 [32, 32, 1152], P(('member', 'lev'), 'lat', 'lon'), parts along dimension 0, may hold values from 0.02 to 0.06
- lon_ahead: float32 [32, 32, 1152], P(('member', 'lev'), 'lat', 'lon'), parts along dimension 0, may hold values from 0.02 to 0.06
- lon_behind: float32 [32, 32, 1152], P(('member', 'lev'), 'lat', 'lon'), parts along dimension 0, may hold values from 0.02 to 0.06
- coupling: float32 [16, 5, 5], P('lev'), may hold values from -0.9 to 0.9
- cutoff: int32 [32], replicated, may hold values from 1 to 576, as said below
Outputs:
- adjoint_out: float32 [10, 16, 32, 1152], P('member', 'lev', 'lat', 'lon'), parts along dimension 0
The draws below stay inside these ranges and needn't reach their ends.
There are 2 independent parts, one for each index of `member`. The reference program is written for one: setup_inputs(seed, part) draws one part's arguments, and reference() takes and returns one part's arrays. A program takes and returns all parts, laid end to end along the dimension named above; an argument that names none is the same for every part. Nothing has to cross between parts.
Inputs may be any that keep to these rules, and one draw needn't show every extreme that they name: Rows 8 to 23 have a cutoff of exactly 576, every other row a cutoff below 576; the first and the last row have cutoff 1.
All inputs are finite; a program needn't handle non-finite values.
Results may differ from the reference program's by a relative error of at most 0.00011.
Values sent between devices are 32-bit elements; how exact they have to be, the bound alone decides.
A program may use at most 64 MiB of HBM per device.

```python
import math
import jax
import jax.numpy as jnp
from jax import lax

NLON = 1152
FIELDS = 5
SUBSTEPS = 6
NLAT = 32
LEVELS = 16


def draw_cutoff(key, part):
    row_index = jnp.arange(NLAT, dtype=jnp.int32)
    is_polar = (row_index < NLAT // 4) | (row_index >= 3 * NLAT // 4)
    drawn = jax.random.randint(key, (NLAT,), 1, NLON // 2, dtype=jnp.int32)
    drawn = jnp.where((row_index == 0) | (row_index == NLAT - 1), 1, drawn)
    return jnp.where(is_polar, drawn, NLON // 2).astype(jnp.int32)


def level_of(own_key, shape, cuts, least, largest):
    def one(dim, shards_of):
        steps = jax.random.uniform(jax.random.fold_in(jax.random.fold_in(own_key, 6), dim), (shards_of,), jnp.float32, least / len(cuts), largest / len(cuts))
        return jnp.repeat(jnp.exp(steps), shape[dim] // shards_of).reshape((-1,) + (1,) * (len(shape) - dim - 1))

    level = one(*cuts[0])
    for cut in cuts[1:]:
        level = level * one(*cut)
    return level


def centred(own_key, shape, deviation, most, pieces=(), kind=jnp.bfloat16):
    loudness = level_of(own_key, shape, pieces, -0.22, 0.18) if pieces else 1.0
    result = jax.random.normal(own_key, shape, jnp.float32) * deviation * loudness
    return jnp.minimum(jnp.maximum(result, -most), most).astype(kind)


def setup_inputs(seed: int = 0, part: int = 0) -> dict:
    keys = jax.random.split(jax.random.key(seed), 8)
    part_splits = jax.random.split(jax.random.fold_in(keys[7], part), 8)
    adjoint_in = centred(part_splits[0], (FIELDS, LEVELS, NLAT, NLON), 2.0, 12.0, ((1, 2), (2, 4), (3, 2)), jnp.float32)
    lat_ahead = jnp.clip(jnp.exp(math.log(0.8) - 0.82667861 * jax.random.uniform(part_splits[1], (LEVELS, NLAT, NLON), jnp.float32) ** level_of(part_splits[1], (LEVELS, NLAT, NLON), ((0, 2), (1, 4), (2, 2)), -0.2, 0.2)), 0.35, 0.8)
    lat_behind = jnp.clip(jnp.exp(math.log(0.06) - 1.0986123 * jax.random.uniform(part_splits[2], (LEVELS, NLAT, NLON), jnp.float32) ** level_of(part_splits[2], (LEVELS, NLAT, NLON), ((0, 2), (1, 4), (2, 2)), -0.2, 0.2)), 0.02, 0.06)
    lon_ahead = jnp.clip(jnp.exp(math.log(0.06) - 1.0986123 * jax.random.uniform(part_splits[3], (LEVELS, NLAT, NLON), jnp.float32) ** level_of(part_splits[3], (LEVELS, NLAT, NLON), ((0, 2), (1, 4), (2, 2)), -0.2, 0.2)), 0.02, 0.06)
    lon_behind = jnp.clip(jnp.exp(math.log(0.06) - 1.0986123 * jax.random.uniform(part_splits[4], (LEVELS, NLAT, NLON), jnp.float32) ** level_of(part_splits[4], (LEVELS, NLAT, NLON), ((0, 2), (1, 4), (2, 2)), -0.2, 0.2)), 0.02, 0.06)
    coupling = centred(keys[5], (LEVELS, FIELDS, FIELDS), 0.15, 0.9, ((0, 2),), jnp.float32)
    cutoff = draw_cutoff(jax.random.fold_in(keys[7], 71), part)
    return dict(adjoint_in=adjoint_in, lat_ahead=lat_ahead, lat_behind=lat_behind, lon_ahead=lon_ahead, lon_behind=lon_behind, coupling=coupling, cutoff=cutoff)


def damping_table(cutoff):
    wavenumber = jnp.arange(NLON // 2 + 1).astype(jnp.float32)
    limit = cutoff.astype(jnp.float32)[:, None]
    ratio = limit / jnp.maximum(wavenumber, 1.0)[None, :]
    return jnp.where(wavenumber[None, :] > limit, ratio * ratio, 1.0)


def polar_filter(field_block, damping):
    spectra = jnp.fft.rfft(field_block, axis=-1)
    return jnp.fft.irfft(spectra * damping, n=NLON, axis=-1).astype(jnp.float32)


def reference(adjoint_in, lat_ahead, lat_behind, lon_ahead, lon_behind, coupling, cutoff):
    damping = damping_table(cutoff)
    current = jnp.stack([polar_filter(adjoint_in[field_index], damping) for field_index in range(FIELDS)])
    row_mask = (jnp.arange(NLAT) < NLAT - 1).astype(jnp.float32)[None, :, None]
    north_rate = lat_ahead * row_mask
    zero_row = jnp.zeros((LEVELS, 1, NLON), jnp.float32)
    south_rate = jnp.concatenate([zero_row, lat_behind[:, :-1]], axis=1)
    east_rate = lon_ahead
    west_rate = jnp.roll(lon_behind, 1, axis=2)
    zero_plane = jnp.zeros((FIELDS, LEVELS, 1, NLON), jnp.float32)
    for substep in range(SUBSTEPS):
        current = current + jnp.einsum("lgf,glji->flji", coupling, current, precision=lax.Precision.HIGHEST)
        north_side = jnp.concatenate([current[:, :, 1:], zero_plane], axis=2)
        south_side = jnp.concatenate([zero_plane, current[:, :, :-1]], axis=2)
        east_side = jnp.roll(current, -1, axis=3)
        west_side = jnp.roll(current, 1, axis=3)
        current = (current + east_rate * (east_side - current) + west_rate * (west_side - current)
                   + north_rate * (north_side - current) + south_rate * (south_side - current))
    return current
```

```python
import functools

import jax
import jax.numpy as jnp
import numpy as np
from jax import lax
from jax.experimental import pallas as pl
from jax.experimental.pallas import tpu as pltpu
from jax.sharding import PartitionSpec as P

SUBSTEPS = 6
DEPTH = 1
RIM = 16
LANES = 128
MESH = pl.DeviceIdType.MESH


def split_parts(table):
    high = table.astype(jnp.bfloat16)
    low = (table - high.astype(np.float32)).astype(jnp.bfloat16)
    return np.stack([high, low])


def tables(circle, sector, width):
    column = np.arange(circle)
    middle = circle // 2
    wavenumber = np.where(column <= middle, column, column - middle)
    position = np.arange(circle)
    phase = (position[:, None] * wavenumber[None, :]) % circle
    angle = phase * (2.0 * np.pi / circle)
    weight = np.where((column == 0) | (column == middle), 1.0 / circle, 2.0 / circle)
    basis = np.where((column <= middle)[None, :], np.cos(angle), np.sin(angle))
    basis = (basis * np.sqrt(weight)[None, :]).astype(np.float32)
    lane = np.arange(width)
    target = np.where(lane < sector + RIM, lane, lane - width) % circle
    return split_parts(basis), split_parts(np.ascontiguousarray(basis[target].T)), wavenumber


def halves(values):
    high = values.astype(jnp.bfloat16)
    low = (values - high.astype(jnp.float32)).astype(jnp.bfloat16)
    return high, low


def product(values, high_table, low_table):
    high, low = halves(values)
    dot = functools.partial(jnp.dot, preferred_element_type=jnp.float32)
    return dot(high, high_table) + (dot(high, low_table) + dot(low, high_table))


def kernel(
    peers, bands, fields, rows, levels, sector, width,
    x_ref, rate_refs, couple_ref, damp_ref, forward_hbm, inverse_hbm, out_ref,
    forward, inverse, swapped, spectra, filtered, rate_rows, packed, rim, rates, coefs, power, state,
    table_sem, swap_send, swap_recv, rim_send, rim_recv, rate_send, rate_recv, edge_send, edge_recv,
):
    chunks = 2
    lat = lax.axis_index("lat")
    lon = lax.axis_index("lon")
    quarter = bands // 4
    polar = (lat < quarter) | (lat >= 3 * quarter)
    has_prev = lat > 0
    has_next = lat < bands - 1
    plane = rows * levels
    part = plane // chunks
    tail = sector % LANES
    body = sector - tail

    def lon_id(d):
        return {"lon": lax.rem(lon + d + peers, peers)}

    barrier = pltpu.get_barrier_semaphore()
    for d in range(1, peers):
        pl.semaphore_signal(barrier, inc=1, device_id=lon_id(d), device_id_type=MESH)

    @pl.when(has_prev)
    def _():
        pl.semaphore_signal(barrier, inc=1, device_id={"lat": lat - 1}, device_id_type=MESH)

    @pl.when(has_next)
    def _():
        pl.semaphore_signal(barrier, inc=1, device_id={"lat": lat + 1}, device_id_type=MESH)

    table_copies = [
        pltpu.make_async_copy(forward_hbm, forward, table_sem.at[0]),
        pltpu.make_async_copy(inverse_hbm, inverse, table_sem.at[1]),
    ]

    @pl.when(polar)
    def _():
        for copy in table_copies:
            copy.start()

    sources = [r for r in rate_refs] + [x_ref.at[f] for f in range(fields)]
    lane = lax.broadcasted_iota(jnp.int32, (plane, LANES), 1)
    for block in range(packed.shape[0]):
        value = jnp.zeros((plane, LANES), jnp.float32)
        for k, source in enumerate(sources[4 * block:4 * block + 4]):
            first = source[:, 0:LANES]
            last = jnp.concatenate(
                [source[:, body:sector], jnp.zeros((plane, LANES - tail), jnp.float32)], axis=1
            )
            base = 32 * k
            if base:
                first = pltpu.roll(first, base, 1)
            last = pltpu.roll(last, (base + RIM - (tail - RIM)) % LANES, 1)
            value = jnp.where((lane >= base) & (lane < base + RIM), first, value)
            value = jnp.where((lane >= base + RIM) & (lane < base + 2 * RIM), last, value)
        packed[block] = value

    greeters = peers - 1 + has_prev.astype(jnp.int32) + has_next.astype(jnp.int32)
    pl.semaphore_wait(barrier, greeters)

    rim_slots = rim.shape[0]
    rim_copies = [
        pltpu.make_async_remote_copy(
            src_ref=packed, dst_ref=rim.at[slot], send_sem=rim_send.at[slot],
            recv_sem=rim_recv.at[slot], device_id=lon_id(-1 if slot == 0 else 1), device_id_type=MESH,
        )
        for slot in range(rim_slots)
    ]
    for copy in rim_copies:
        copy.start()

    swaps = [
        [
            pltpu.make_async_remote_copy(
                src_ref=x_ref.at[:, pl.ds(c * part, part)],
                dst_ref=swapped.at[d - 1, :, pl.ds(c * part, part)],
                send_sem=swap_send.at[c, d - 1], recv_sem=swap_recv.at[c, d - 1],
                device_id=lon_id(-d), device_id_type=MESH,
            )
            for d in range(1, peers)
        ]
        for c in range(chunks)
    ]

    @pl.when(polar)
    def _():
        for c in range(chunks):
            for copy in swaps[c]:
                copy.start()

    def entry(g, f):
        value = couple_ref[g * fields + f]
        return value + 1.0 if g == f else value

    once = [[entry(g, f) for f in range(fields)] for g in range(fields)]

    def multiply(a, b):
        return [
            [sum(a[g][h] * b[h][f] for h in range(fields)) for f in range(fields)]
            for g in range(fields)
        ]

    result = once
    for _ in range(SUBSTEPS - 1):
        result = multiply(result, once)
    for g in range(fields):
        for f in range(fields):
            power[g * fields + f] = result[g][f]

    depth = DEPTH

    @pl.when(jnp.logical_not(has_prev))
    def _():
        rates[:, 0:depth] = jnp.zeros((4, depth, levels, width), jnp.float32)
        for s in range(0, SUBSTEPS, depth):
            state[s, :, 0:depth] = jnp.zeros((fields, depth, levels, width), jnp.float32)

    @pl.when(jnp.logical_not(has_next))
    def _():
        rates[:, depth + rows:] = jnp.zeros((4, depth, levels, width), jnp.float32)
        for s in range(0, SUBSTEPS, depth):
            state[s, :, depth + rows:] = jnp.zeros((fields, depth, levels, width), jnp.float32)

    for copy in rim_copies:
        copy.wait()

    def with_rim(index, target):
        source = sources[index]
        block, base = index // 4, 32 * (index % 4)
        east = pltpu.roll(rim[0, block], (tail - base) % LANES, 1)
        west = pltpu.roll(rim[rim_slots - 1, block], (LANES - RIM - base - RIM) % LANES, 1)
        last = jnp.concatenate(
            [source[:, body:sector], jnp.zeros((plane, LANES - tail), jnp.float32)], axis=1
        )
        last = jnp.where((lane >= tail) & (lane < tail + RIM), east, last)
        last = jnp.where(lane >= LANES - RIM, west, last)
        for t in range(body // LANES):
            target[t] = source[:, t * LANES:(t + 1) * LANES]
        target[body // LANES] = last

    def row_of(ref, j):
        return jnp.concatenate(
            [ref[t, pl.ds(j, levels, rows), :] for t in range(width // LANES)], axis=1
        )

    for r in range(4):
        with_rim(r, rate_rows.at[r])
    for r in range(4):
        for j in range(rows):
            rates[r, depth + j] = row_of(rate_rows.at[r], j)

    def to_neighbours(ref, send, recv):
        to_prev = pltpu.make_async_remote_copy(
            src_ref=ref.at[:, pl.ds(depth, depth)], dst_ref=ref.at[:, pl.ds(depth + rows, depth)],
            send_sem=send.at[0], recv_sem=recv.at[0],
            device_id={"lat": lat - 1}, device_id_type=MESH,
        )
        to_next = pltpu.make_async_remote_copy(
            src_ref=ref.at[:, pl.ds(rows, depth)], dst_ref=ref.at[:, pl.ds(0, depth)],
            send_sem=send.at[1], recv_sem=recv.at[1],
            device_id={"lat": lat + 1}, device_id_type=MESH,
        )

        def start():
            pl.when(has_prev)(to_prev.start)
            pl.when(has_next)(to_next.start)

        def arrive():
            pl.when(has_next)(to_prev.wait_recv)
            pl.when(has_prev)(to_next.wait_recv)

        def sent():
            pl.when(has_prev)(to_prev.wait_send)
            pl.when(has_next)(to_next.wait_send)

        return start, arrive, sent

    rate_start, rate_arrive, rate_sent = to_neighbours(rates, rate_send, rate_recv)
    rate_start()

    @pl.when(jnp.logical_not(polar))
    def _():
        for f in range(fields):
            with_rim(4 + f, filtered.at[f])

    modes = peers * sector

    @pl.when(polar)
    def _():
        for copy in table_copies:
            copy.wait()
        for c in range(chunks):
            own = x_ref[:, c * part:(c + 1) * part].reshape(fields * part, sector)
            spectra[c] = product(own, forward[0, 0:sector], forward[1, 0:sector])
        for c in range(chunks):
            for copy in swaps[c]:
                copy.wait_recv()
            total = spectra[c]
            for d in range(1, peers):
                values = swapped[d - 1, :, c * part:(c + 1) * part].reshape(fields * part, sector)
                start, end = d * sector, (d + 1) * sector
                total = total + product(values, forward[0, start:end], forward[1, start:end])
            damped = total.reshape(fields * part // rows, rows, modes) * damp_ref[...][None]
            result = product(damped.reshape(fields * part, modes), inverse[0], inverse[1])
            for t in range(width // LANES):
                block = result[:, t * LANES:(t + 1) * LANES].reshape(fields, part, LANES)
                filtered[:, t, c * part:(c + 1) * part] = block

    edges = [
        to_neighbours(state.at[s], edge_send.at[s // depth], edge_recv.at[s // depth])
        for s in range(0, SUBSTEPS, depth)
    ]

    def couple(j):
        values = [row_of(filtered.at[g], j) for g in range(fields)]
        for f in range(fields):
            total = None
            for g in range(fields):
                term = jnp.tile(power[g * fields + f], (1, width // LANES)) * values[g]
                total = term if total is None else total + term
            state[0, f, depth + j] = total

    outer = list(range(depth)) + list(range(rows - depth, rows))
    inner = list(range(depth, rows - depth))
    for j in outer:
        couple(j)
    edges[0][0]()
    for j in inner:
        couple(j)

    rate_arrive()
    below_last = jnp.where(has_next, 1.0, 0.0)
    for j in range(1, rows + 2 * depth - 1):
        north = rates[0, j]
        if j == depth + rows - 1:
            north = north * below_last
        south = rates[1, j - 1]
        east = rates[2, j]
        west = pltpu.roll(rates[3, j], 1, 1)
        coefs[0, j] = 1.0 - east - west - north - south
        coefs[1, j] = east
        coefs[2, j] = west
        coefs[3, j] = north
        coefs[4, j] = south

    def advance(s, j):
        rate = [coefs[k, j] for k in range(5)]
        for f in range(fields):
            here = state[s, f, j]
            value = (
                rate[0] * here
                + rate[1] * pltpu.roll(here, width - 1, 1)
                + rate[2] * pltpu.roll(here, 1, 1)
                + rate[3] * state[s, f, j + 1]
                + rate[4] * state[s, f, j - 1]
            )
            state[s + 1, f, j] = value

    def advance_rows(s, start, end):
        if end > start:
            @pl.loop(start, end)
            def _(j):
                advance(s, j)

    for s in range(SUBSTEPS):
        reach = depth - 1 - s % depth
        begin, end = depth - reach, depth + rows + reach
        if s % depth == 0:
            edges[s // depth][1]()
        if (s + 1) % depth == 0 and s + 1 < SUBSTEPS:
            advance_rows(s, depth, 2 * depth)
            advance_rows(s, rows, rows + depth)
            edges[(s + 1) // depth][0]()
            advance_rows(s, 2 * depth, rows)
        else:
            advance_rows(s, begin, end)

    for f in range(fields):
        for j in range(rows):
            value = state[SUBSTEPS, f, depth + j]
            for t in range(width // LANES):
                filtered[f, t, pl.ds(j, levels, rows), :] = value[:, t * LANES:(t + 1) * LANES]
    for t in range(width // LANES):
        end = min(sector, (t + 1) * LANES)
        out_ref[:, :, t * LANES:end] = filtered[:, t, :, 0:end - t * LANES]

    rate_sent()
    for edge in edges:
        edge[2]()

    @pl.when(polar)
    def _():
        for c in range(chunks):
            for copy in swaps[c]:
                copy.wait_send()


def shards(peers, bands, adjoint_in, lat_ahead, lat_behind, lon_ahead, lon_behind, coupling, cutoff):
    fields, levels, rows, sector = adjoint_in.shape
    width = -(-(sector + 2 * RIM) // LANES) * LANES
    circle = sector * peers
    forward, inverse, wavenumber = tables(circle, sector, width)
    plane = rows * levels
    limits = lax.dynamic_slice_in_dim(cutoff, lax.axis_index("lat") * rows, rows, 0)
    limit = limits.astype(jnp.float32)[:, None]
    number = jnp.asarray(wavenumber, jnp.float32)[None, :]
    ratio = limit / jnp.maximum(number, 1.0)
    damping = jnp.where(number > limit, ratio * ratio, 1.0)
    couple = jnp.broadcast_to(
        jnp.transpose(coupling, (1, 2, 0)).reshape(fields * fields, levels, 1), (fields * fields, levels, LANES)
    )
    flat = [r.reshape(plane, sector) for r in (lat_ahead, lat_behind, lon_ahead, lon_behind)]
    vmem = pl.BlockSpec(memory_space=pltpu.VMEM)
    anywhere = pl.BlockSpec(memory_space=pl.ANY)
    rim_slots = 1 if peers == 2 else 2
    packs = -(-(4 + fields) // 4)
    tall = rows + 2 * DEPTH
    rounds = SUBSTEPS // DEPTH

    def body(x, a, b, c, d, *rest):
        kernel(peers, bands, fields, rows, levels, sector, width, x, [a, b, c, d], *rest)

    dma = pltpu.SemaphoreType.DMA
    out = pl.pallas_call(
        body,
        out_shape=jax.ShapeDtypeStruct((fields, plane, sector), jnp.float32),
        in_specs=[vmem] * 7 + [anywhere] * 2,
        out_specs=vmem,
        scratch_shapes=[
            pltpu.VMEM(forward.shape, jnp.bfloat16),
            pltpu.VMEM(inverse.shape, jnp.bfloat16),
            pltpu.VMEM((peers - 1, fields, plane, sector), jnp.float32),
            pltpu.VMEM((2, fields * plane // 2, circle), jnp.float32),
            pltpu.VMEM((fields, width // LANES, plane, LANES), jnp.float32),
            pltpu.VMEM((4, width // LANES, plane, LANES), jnp.float32),
            pltpu.VMEM((packs, plane, LANES), jnp.float32),
            pltpu.VMEM((rim_slots, packs, plane, LANES), jnp.float32),
            pltpu.VMEM((4, tall, levels, width), jnp.float32),
            pltpu.VMEM((5, tall, levels, width), jnp.float32),
            pltpu.VMEM((fields * fields, levels, LANES), jnp.float32),
            pltpu.VMEM((SUBSTEPS + 1, fields, tall, levels, width), jnp.float32),
            dma((2,)), dma((2, peers - 1)), dma((2, peers - 1)),
            dma((rim_slots,)), dma((rim_slots,)),
            dma((2,)), dma((2,)), dma((rounds, 2)), dma((rounds, 2)),
        ],
        compiler_params=pltpu.CompilerParams(
            collective_id=0, has_side_effects=True, vmem_limit_bytes=48 * 1024 * 1024
        ),
    )(adjoint_in.reshape(fields, plane, sector), *flat, couple, damping, jnp.asarray(forward), jnp.asarray(inverse))
    return out.reshape(fields, levels, rows, sector)


def solution(mesh):
    placed = (
        P("member", "lev", "lat", "lon"),
        P(("member", "lev"), "lat", "lon"),
        P(("member", "lev"), "lat", "lon"),
        P(("member", "lev"), "lat", "lon"),
        P(("member", "lev"), "lat", "lon"),
        P("lev", None, None),
        P(),
    )
    return jax.shard_map(
        functools.partial(shards, mesh.shape["lon"], mesh.shape["lat"]),
        mesh=mesh,
        in_specs=placed,
        out_specs=P("member", "lev", "lat", "lon"),
        check_vma=False,
    )
```

```python
import functools

import jax
import jax.numpy as jnp
import numpy as np
from jax import lax
from jax.experimental import pallas as pl
from jax.experimental.pallas import tpu as pltpu
from jax.sharding import PartitionSpec as P

SUBSTEPS = 6
DEPTH = 3
RIM = 16
LANES = 128
MESH = pl.DeviceIdType.MESH


def split_parts(table):
    high = table.astype(jnp.bfloat16)
    low = (table - high.astype(np.float32)).astype(jnp.bfloat16)
    return np.stack([high, low])


def tables(circle, sector, width):
    column = np.arange(circle)
    middle = circle // 2
    wavenumber = np.where(column <= middle, column, column - middle)
    position = np.arange(circle)
    phase = (position[:, None] * wavenumber[None, :]) % circle
    angle = phase * (2.0 * np.pi / circle)
    weight = np.where((column == 0) | (column == middle), 1.0 / circle, 2.0 / circle)
    basis = np.where((column <= middle)[None, :], np.cos(angle), np.sin(angle))
    basis = (basis * np.sqrt(weight)[None, :]).astype(np.float32)
    lane = np.arange(width)
    target = np.where(lane < sector + RIM, lane, lane - width) % circle
    return split_parts(basis), split_parts(np.ascontiguousarray(basis[target].T))


def halves(values):
    high = values.astype(jnp.bfloat16)
    low = (values - high.astype(jnp.float32)).astype(jnp.bfloat16)
    return high, low


def product(values, high_table, low_table):
    high, low = halves(values)
    dot = functools.partial(jnp.dot, preferred_element_type=jnp.float32)
    return dot(high, high_table) + (dot(high, low_table) + dot(low, high_table))


def kernel(
    peers, bands, fields, rows, levels, sector, width,
    x_hbm, rates_hbm, couple_ref, cutoff_ref, forward_hbm, inverse_hbm, out_ref,
    x_ref, rate_ref, forward, inverse, swapped, spectra, filtered, rate_rows, packed, rim, rates, coefs, power, state, damp_ref,
    load_sem, table_sem, swap_send, swap_recv, rim_send, rim_recv, rate_send, rate_recv, edge_send, edge_recv,
):
    chunks = 2
    lat = lax.axis_index("lat")
    lon = lax.axis_index("lon")
    quarter = bands // 4
    polar = (lat < quarter) | (lat >= 3 * quarter)
    has_prev = lat > 0
    has_next = lat < bands - 1
    plane = rows * levels
    part = plane // chunks
    tail = sector % LANES
    body = sector - tail

    def lon_id(d):
        return {"lon": lax.rem(lon + d + peers, peers)}

    barrier = pltpu.get_barrier_semaphore()
    for d in range(1, peers):
        pl.semaphore_signal(barrier, inc=1, device_id=lon_id(d), device_id_type=MESH)

    @pl.when(has_prev)
    def _():
        pl.semaphore_signal(barrier, inc=1, device_id={"lat": lat - 1}, device_id_type=MESH)

    @pl.when(has_next)
    def _():
        pl.semaphore_signal(barrier, inc=1, device_id={"lat": lat + 1}, device_id_type=MESH)

    rate_refs = [rate_ref.at[r] for r in range(4)]
    loads = [pltpu.make_async_copy(x_hbm, x_ref, load_sem.at[4])]
    loads += [pltpu.make_async_copy(rates_hbm[r], rate_ref.at[r], load_sem.at[r]) for r in range(4)]
    for copy in loads:
        copy.start()

    table_copies = [
        pltpu.make_async_copy(forward_hbm, forward, table_sem.at[0]),
        pltpu.make_async_copy(inverse_hbm, inverse, table_sem.at[1]),
    ]

    @pl.when(polar)
    def _():
        for copy in table_copies:
            copy.start()

    greeters = peers - 1 + has_prev.astype(jnp.int32) + has_next.astype(jnp.int32)
    pl.semaphore_wait(barrier, greeters)

    swaps = [
        [
            pltpu.make_async_remote_copy(
                src_ref=x_hbm.at[:, pl.ds(c * part, part)],
                dst_ref=swapped.at[d - 1, :, pl.ds(c * part, part)],
                send_sem=swap_send.at[c, d - 1], recv_sem=swap_recv.at[c, d - 1],
                device_id=lon_id(-d), device_id_type=MESH,
            )
            for d in range(1, peers)
        ]
        for c in range(chunks)
    ]

    @pl.when(polar)
    def _():
        for copy in swaps[0]:
            copy.start()

    for copy in loads:
        copy.wait()

    sources = [r for r in rate_refs] + [x_ref.at[f] for f in range(fields)]
    lane = lax.broadcasted_iota(jnp.int32, (plane, LANES), 1)
    for block in range(packed.shape[0]):
        value = jnp.zeros((plane, LANES), jnp.float32)
        for k, source in enumerate(sources[4 * block:4 * block + 4]):
            first = source[:, 0:LANES]
            last = jnp.concatenate(
                [source[:, body:sector], jnp.zeros((plane, LANES - tail), jnp.float32)], axis=1
            )
            base = 32 * k
            if base:
                first = pltpu.roll(first, base, 1)
            last = pltpu.roll(last, (base + RIM - (tail - RIM)) % LANES, 1)
            value = jnp.where((lane >= base) & (lane < base + RIM), first, value)
            value = jnp.where((lane >= base + RIM) & (lane < base + 2 * RIM), last, value)
        packed[block] = value

    rim_slots = rim.shape[0]

    def rim_copies(stage, start, stop):
        return [
            pltpu.make_async_remote_copy(
                src_ref=packed.at[start:stop], dst_ref=rim.at[slot, start:stop],
                send_sem=rim_send.at[stage, slot], recv_sem=rim_recv.at[stage, slot],
                device_id=lon_id(-1 if slot == 0 else 1), device_id_type=MESH,
            )
            for slot in range(rim_slots)
        ]

    rate_rims, field_rims = rim_copies(0, 0, 1), rim_copies(1, 1, packed.shape[0])
    for copy in rate_rims:
        copy.start()

    @pl.when(polar)
    def _():
        for c in range(1, chunks):
            for copy in swaps[c]:
                copy.start()

    @pl.when(jnp.logical_not(polar))
    def _():
        for copy in field_rims:
            copy.start()

    level_of = lax.broadcasted_iota(jnp.int32, (levels, LANES), 0)

    def entry(g, f):
        value = jnp.full((levels, LANES), 1.0 if g == f else 0.0, jnp.float32)
        for level in range(levels):
            value = jnp.where(level_of == level, value + couple_ref[level * fields * fields + g * fields + f], value)
        return value

    once = [[entry(g, f) for f in range(fields)] for g in range(fields)]

    def multiply(a, b):
        return [
            [sum(a[g][h] * b[h][f] for h in range(fields)) for f in range(fields)]
            for g in range(fields)
        ]

    result = once
    for _ in range(SUBSTEPS - 1):
        result = multiply(result, once)
    for g in range(fields):
        for f in range(fields):
            power[g * fields + f] = result[g][f]

    depth = DEPTH

    @pl.when(jnp.logical_not(has_prev))
    def _():
        rates[:, 0:depth] = jnp.zeros((4, depth, levels, width), jnp.float32)
        for s in range(0, SUBSTEPS, depth):
            state[s, :, 0:depth] = jnp.zeros((fields, depth, levels, width), jnp.float32)

    @pl.when(jnp.logical_not(has_next))
    def _():
        rates[:, depth + rows:] = jnp.zeros((4, depth, levels, width), jnp.float32)
        for s in range(0, SUBSTEPS, depth):
            state[s, :, depth + rows:] = jnp.zeros((fields, depth, levels, width), jnp.float32)

    for copy in rate_rims:
        copy.wait()

    def with_rim(index, target):
        source = sources[index]
        block, base = index // 4, 32 * (index % 4)
        east = pltpu.roll(rim[0, block], (tail - base) % LANES, 1)
        west = pltpu.roll(rim[rim_slots - 1, block], (LANES - RIM - base - RIM) % LANES, 1)
        last = jnp.concatenate(
            [source[:, body:sector], jnp.zeros((plane, LANES - tail), jnp.float32)], axis=1
        )
        last = jnp.where((lane >= tail) & (lane < tail + RIM), east, last)
        last = jnp.where(lane >= LANES - RIM, west, last)
        for t in range(body // LANES):
            target[t] = source[:, t * LANES:(t + 1) * LANES]
        target[body // LANES] = last

    def row_of(ref, j):
        return jnp.concatenate(
            [ref[t, pl.ds(j, levels, rows), :] for t in range(width // LANES)], axis=1
        )

    for r in range(4):
        with_rim(r, rate_rows.at[r])
    for r in range(4):
        for j in range(rows):
            rates[r, depth + j] = row_of(rate_rows.at[r], j)

    def to_neighbours(ref, send, recv):
        to_prev = pltpu.make_async_remote_copy(
            src_ref=ref.at[:, pl.ds(depth, depth)], dst_ref=ref.at[:, pl.ds(depth + rows, depth)],
            send_sem=send.at[0], recv_sem=recv.at[0],
            device_id={"lat": lat - 1}, device_id_type=MESH,
        )
        to_next = pltpu.make_async_remote_copy(
            src_ref=ref.at[:, pl.ds(rows, depth)], dst_ref=ref.at[:, pl.ds(0, depth)],
            send_sem=send.at[1], recv_sem=recv.at[1],
            device_id={"lat": lat + 1}, device_id_type=MESH,
        )

        def start():
            pl.when(has_prev)(to_prev.start)
            pl.when(has_next)(to_next.start)

        def arrive():
            pl.when(has_next)(to_prev.wait_recv)
            pl.when(has_prev)(to_next.wait_recv)

        def sent():
            pl.when(has_prev)(to_prev.wait_send)
            pl.when(has_next)(to_next.wait_send)

        return start, arrive, sent

    rate_start, rate_arrive, rate_sent = to_neighbours(rates, rate_send, rate_recv)
    rate_start()

    @pl.when(jnp.logical_not(polar))
    def _():
        for copy in field_rims:
            copy.wait()
        for f in range(fields):
            with_rim(4 + f, filtered.at[f])

    modes = peers * sector

    @pl.when(polar)
    def _():
        column = lax.broadcasted_iota(jnp.int32, (rows, modes), 1)
        row_index = lax.broadcasted_iota(jnp.int32, (rows, modes), 0)
        number = jnp.where(column <= modes // 2, column, column - modes // 2).astype(jnp.float32)
        limit = jnp.zeros((rows, modes), jnp.float32)
        for j in range(rows):
            limit = jnp.where(row_index == j, cutoff_ref[lat * rows + j].astype(jnp.float32), limit)
        ratio = limit / jnp.maximum(number, 1.0)
        damp_ref[...] = jnp.where(number > limit, ratio * ratio, 1.0)
        for copy in table_copies:
            copy.wait()
        for c in range(chunks):
            own = x_ref[:, c * part:(c + 1) * part].reshape(fields * part, sector)
            spectra[c] = product(own, forward[0, 0:sector], forward[1, 0:sector])
        for c in range(chunks):
            for copy in swaps[c]:
                copy.wait_recv()
            total = spectra[c]
            for d in range(1, peers):
                values = swapped[d - 1, :, c * part:(c + 1) * part].reshape(fields * part, sector)
                start, end = d * sector, (d + 1) * sector
                total = total + product(values, forward[0, start:end], forward[1, start:end])
            damped = total.reshape(fields * part // rows, rows, modes) * damp_ref[...][None]
            result = product(damped.reshape(fields * part, modes), inverse[0], inverse[1])
            for t in range(width // LANES):
                block = result[:, t * LANES:(t + 1) * LANES].reshape(fields, part, LANES)
                filtered[:, t, c * part:(c + 1) * part] = block

    edges = [
        to_neighbours(state.at[s], edge_send.at[s // depth], edge_recv.at[s // depth])
        for s in range(0, SUBSTEPS, depth)
    ]

    def couple(j):
        values = [row_of(filtered.at[g], j) for g in range(fields)]
        for f in range(fields):
            total = None
            for g in range(fields):
                term = jnp.tile(power[g * fields + f], (1, width // LANES)) * values[g]
                total = term if total is None else total + term
            state[0, f, depth + j] = total

    outer = list(range(depth)) + list(range(rows - depth, rows))
    inner = list(range(depth, rows - depth))
    for j in outer:
        couple(j)
    edges[0][0]()
    for j in inner:
        couple(j)

    rate_arrive()
    below_last = jnp.where(has_next, 1.0, 0.0)
    for j in range(1, rows + 2 * depth - 1):
        north = rates[0, j]
        if j == depth + rows - 1:
            north = north * below_last
        south = rates[1, j - 1]
        east = rates[2, j]
        west = pltpu.roll(rates[3, j], 1, 1)
        coefs[0, j] = 1.0 - east - west - north - south
        coefs[1, j] = east
        coefs[2, j] = west
        coefs[3, j] = north
        coefs[4, j] = south

    def advance(s, j):
        rate = [coefs[k, j] for k in range(5)]
        for f in range(fields):
            here = state[s, f, j]
            value = (
                rate[0] * here
                + rate[1] * pltpu.roll(here, width - 1, 1)
                + rate[2] * pltpu.roll(here, 1, 1)
                + rate[3] * state[s, f, j + 1]
                + rate[4] * state[s, f, j - 1]
            )
            state[s + 1, f, j] = value

    def advance_rows(s, start, end):
        if end > start:
            @pl.loop(start, end)
            def _(j):
                advance(s, j)

    for s in range(SUBSTEPS):
        reach = depth - 1 - s % depth
        begin, end = depth - reach, depth + rows + reach
        if s % depth == 0:
            edges[s // depth][1]()
        if (s + 1) % depth == 0 and s + 1 < SUBSTEPS:
            advance_rows(s, depth, 2 * depth)
            advance_rows(s, rows, rows + depth)
            edges[(s + 1) // depth][0]()
            advance_rows(s, 2 * depth, rows)
        else:
            advance_rows(s, begin, end)

    for f in range(fields):
        for j in range(rows):
            value = state[SUBSTEPS, f, depth + j]
            for t in range(width // LANES):
                filtered[f, t, pl.ds(j, levels, rows), :] = value[:, t * LANES:(t + 1) * LANES]
    for t in range(width // LANES):
        end = min(sector, (t + 1) * LANES)
        out_ref[:, :, t * LANES:end] = filtered[:, t, :, 0:end - t * LANES]

    rate_sent()
    for edge in edges:
        edge[2]()

    @pl.when(polar)
    def _():
        for c in range(chunks):
            for copy in swaps[c]:
                copy.wait_send()


def shards(peers, bands, adjoint_in, lat_ahead, lat_behind, lon_ahead, lon_behind, coupling, cutoff):
    fields, levels, rows, sector = adjoint_in.shape
    width = -(-(sector + 2 * RIM) // LANES) * LANES
    circle = sector * peers
    forward, inverse = tables(circle, sector, width)
    plane = rows * levels
    flat = [r.reshape(plane, sector) for r in (lat_ahead, lat_behind, lon_ahead, lon_behind)]
    vmem = pl.BlockSpec(memory_space=pltpu.VMEM)
    hbm = pl.BlockSpec(memory_space=pltpu.HBM)
    smem = pl.BlockSpec(memory_space=pltpu.SMEM)
    rim_slots = 1 if peers == 2 else 2
    packs = -(-(4 + fields) // 4)
    tall = rows + 2 * DEPTH
    rounds = SUBSTEPS // DEPTH

    def body(x, a, b, c, d, *rest):
        kernel(peers, bands, fields, rows, levels, sector, width, x, [a, b, c, d], *rest)

    dma = pltpu.SemaphoreType.DMA
    out = pl.pallas_call(
        body,
        out_shape=jax.ShapeDtypeStruct((fields, plane, sector), jnp.float32),
        in_specs=[hbm] * 5 + [smem] * 2 + [hbm] * 2,
        out_specs=vmem,
        scratch_shapes=[
            pltpu.VMEM((fields, plane, sector), jnp.float32),
            pltpu.VMEM((4, plane, sector), jnp.float32),
            pltpu.VMEM(forward.shape, jnp.bfloat16),
            pltpu.VMEM(inverse.shape, jnp.bfloat16),
            pltpu.VMEM((peers - 1, fields, plane, sector), jnp.float32),
            pltpu.VMEM((2, fields * plane // 2, circle), jnp.float32),
            pltpu.VMEM((fields, width // LANES, plane, LANES), jnp.float32),
            pltpu.VMEM((4, width // LANES, plane, LANES), jnp.float32),
            pltpu.VMEM((packs, plane, LANES), jnp.float32),
            pltpu.VMEM((rim_slots, packs, plane, LANES), jnp.float32),
            pltpu.VMEM((4, tall, levels, width), jnp.float32),
            pltpu.VMEM((5, tall, levels, width), jnp.float32),
            pltpu.VMEM((fields * fields, levels, LANES), jnp.float32),
            pltpu.VMEM((SUBSTEPS + 1, fields, tall, levels, width), jnp.float32),
            pltpu.VMEM((rows, circle), jnp.float32),
            dma((5,)), dma((2,)), dma((2, peers - 1)), dma((2, peers - 1)),
            dma((2, rim_slots)), dma((2, rim_slots)),
            dma((2,)), dma((2,)), dma((rounds, 2)), dma((rounds, 2)),
        ],
        compiler_params=pltpu.CompilerParams(
            collective_id=0, has_side_effects=True, vmem_limit_bytes=48 * 1024 * 1024
        ),
    )(adjoint_in.reshape(fields, plane, sector), *flat, coupling.reshape(-1), cutoff, jnp.asarray(forward), jnp.asarray(inverse))
    return out.reshape(fields, levels, rows, sector)


def solution(mesh):
    placed = (
        P("member", "lev", "lat", "lon"),
        P(("member", "lev"), "lat", "lon"),
        P(("member", "lev"), "lat", "lon"),
        P(("member", "lev"), "lat", "lon"),
        P(("member", "lev"), "lat", "lon"),
        P("lev", None, None),
        P(),
    )
    return jax.shard_map(
        functools.partial(shards, mesh.shape["lon"], mesh.shape["lat"]),
        mesh=mesh,
        in_specs=placed,
        out_specs=P("member", "lev", "lat", "lon"),
        check_vma=False,
    )
```

```python
import functools

import jax
import jax.numpy as jnp
import numpy as np
from jax import lax
from jax.experimental import pallas as pl
from jax.experimental.pallas import tpu as pltpu
from jax.sharding import PartitionSpec as P

SUBSTEPS = 6
DEPTH = 3
RIM = 16
LANES = 128
VMEM_BYTES = 67_000_000
MESH = pl.DeviceIdType.MESH


def split_parts(table):
    high = table.astype(jnp.bfloat16)
    low = (table - high.astype(np.float32)).astype(jnp.bfloat16)
    return np.stack([high, low])


def tables(circle, sector, width):
    column = np.arange(circle)
    middle = circle // 2
    wavenumber = np.where(column <= middle, column, column - middle)
    position = np.arange(circle)
    phase = (position[:, None] * wavenumber[None, :]) % circle
    angle = phase * (2.0 * np.pi / circle)
    weight = np.where((column == 0) | (column == middle), 1.0 / circle, 2.0 / circle)
    basis = np.where((column <= middle)[None, :], np.cos(angle), np.sin(angle))
    basis = (basis * np.sqrt(weight)[None, :]).astype(np.float32)
    lane = np.arange(width)
    target = np.where(lane < sector + RIM, lane, lane - width) % circle
    return split_parts(basis), split_parts(np.ascontiguousarray(basis[target].T))


def halves(values):
    high = values.astype(jnp.bfloat16)
    low = (values - high.astype(jnp.float32)).astype(jnp.bfloat16)
    return high, low


def product(values, high_table, low_table):
    high, low = halves(values)
    dot = functools.partial(jnp.dot, preferred_element_type=jnp.float32)
    return dot(high, high_table) + (dot(high, low_table) + dot(low, high_table))


def kernel(
    peers, bands, fields, rows, levels, sector, width,
    x_hbm, rates_hbm, couple_ref, cutoff_ref, forward_hbm, inverse_hbm, out_ref,
    x_ref, rate_ref, forward, inverse, swapped, spectra, filtered, rate_rows, packed, rim, rates, coefs, power, state, damp_ref,
    load_sem, table_sem, swap_send, swap_recv, rim_send, rim_recv, rate_send, rate_recv, edge_send, edge_recv,
):
    chunks = 2
    lat = lax.axis_index("lat")
    lon = lax.axis_index("lon")
    quarter = bands // 4
    polar = (lat < quarter) | (lat >= 3 * quarter)
    has_prev = lat > 0
    has_next = lat < bands - 1
    plane = rows * levels
    part = plane // chunks
    tail = sector % LANES
    body = sector - tail

    def lon_id(d):
        return {"lon": lax.rem(lon + d + peers, peers)}

    barrier = pltpu.get_barrier_semaphore()
    for d in range(1, peers):
        pl.semaphore_signal(barrier, inc=1, device_id=lon_id(d), device_id_type=MESH)

    @pl.when(has_prev)
    def _():
        pl.semaphore_signal(barrier, inc=1, device_id={"lat": lat - 1}, device_id_type=MESH)

    @pl.when(has_next)
    def _():
        pl.semaphore_signal(barrier, inc=1, device_id={"lat": lat + 1}, device_id_type=MESH)

    rate_refs = [rate_ref.at[r] for r in range(4)]
    loads = [pltpu.make_async_copy(x_hbm, x_ref, load_sem.at[4])]
    loads += [pltpu.make_async_copy(rates_hbm[r], rate_ref.at[r], load_sem.at[r]) for r in range(4)]
    for copy in loads:
        copy.start()

    table_copies = [
        pltpu.make_async_copy(forward_hbm, forward, table_sem.at[0]),
        pltpu.make_async_copy(inverse_hbm, inverse, table_sem.at[1]),
    ]

    @pl.when(polar)
    def _():
        for copy in table_copies:
            copy.start()

    greeters = peers - 1 + has_prev.astype(jnp.int32) + has_next.astype(jnp.int32)
    pl.semaphore_wait(barrier, greeters)

    swaps = [
        [
            pltpu.make_async_remote_copy(
                src_ref=x_hbm.at[:, pl.ds(c * part, part)],
                dst_ref=swapped.at[d - 1, :, pl.ds(c * part, part)],
                send_sem=swap_send.at[c, d - 1], recv_sem=swap_recv.at[c, d - 1],
                device_id=lon_id(-d), device_id_type=MESH,
            )
            for d in range(1, peers)
        ]
        for c in range(chunks)
    ]

    @pl.when(polar)
    def _():
        for copy in swaps[0]:
            copy.start()

    for copy in loads:
        copy.wait()

    sources = [r for r in rate_refs] + [x_ref.at[f] for f in range(fields)]
    lane = lax.broadcasted_iota(jnp.int32, (plane, LANES), 1)
    for block in range(packed.shape[0]):
        value = jnp.zeros((plane, LANES), jnp.float32)
        for k, source in enumerate(sources[4 * block:4 * block + 4]):
            first = source[:, 0:LANES]
            last = jnp.concatenate(
                [source[:, body:sector], jnp.zeros((plane, LANES - tail), jnp.float32)], axis=1
            )
            base = 32 * k
            if base:
                first = pltpu.roll(first, base, 1)
            last = pltpu.roll(last, (base + RIM - (tail - RIM)) % LANES, 1)
            value = jnp.where((lane >= base) & (lane < base + RIM), first, value)
            value = jnp.where((lane >= base + RIM) & (lane < base + 2 * RIM), last, value)
        packed[block] = value

    rim_slots = rim.shape[0]

    def rim_copies(stage, start, stop):
        return [
            pltpu.make_async_remote_copy(
                src_ref=packed.at[start:stop], dst_ref=rim.at[slot, start:stop],
                send_sem=rim_send.at[stage, slot], recv_sem=rim_recv.at[stage, slot],
                device_id=lon_id(-1 if slot == 0 else 1), device_id_type=MESH,
            )
            for slot in range(rim_slots)
        ]

    rate_rims, field_rims = rim_copies(0, 0, 1), rim_copies(1, 1, packed.shape[0])
    for copy in rate_rims:
        copy.start()

    @pl.when(polar)
    def _():
        for c in range(1, chunks):
            for copy in swaps[c]:
                copy.start()

    @pl.when(jnp.logical_not(polar))
    def _():
        for copy in field_rims:
            copy.start()

    def entry(g, f):
        value = jnp.broadcast_to(couple_ref[g, :, f:f + 1], (levels, LANES))
        return value + 1.0 if g == f else value

    once = [[entry(g, f) for f in range(fields)] for g in range(fields)]

    def multiply(a, b):
        return [
            [sum(a[g][h] * b[h][f] for h in range(fields)) for f in range(fields)]
            for g in range(fields)
        ]

    result = once
    for _ in range(SUBSTEPS - 1):
        result = multiply(result, once)
    for g in range(fields):
        for f in range(fields):
            power[g * fields + f] = result[g][f]

    depth = DEPTH

    @pl.when(jnp.logical_not(has_prev))
    def _():
        rates[:, 0:depth] = jnp.zeros((4, depth, levels, width), jnp.float32)
        for s in range(0, SUBSTEPS, depth):
            state[s, :, 0:depth] = jnp.zeros((fields, depth, levels, width), jnp.float32)

    @pl.when(jnp.logical_not(has_next))
    def _():
        rates[:, depth + rows:] = jnp.zeros((4, depth, levels, width), jnp.float32)
        for s in range(0, SUBSTEPS, depth):
            state[s, :, depth + rows:] = jnp.zeros((fields, depth, levels, width), jnp.float32)

    for copy in rate_rims:
        copy.wait()

    def with_rim(index, target):
        source = sources[index]
        block, base = index // 4, 32 * (index % 4)
        east = pltpu.roll(rim[0, block], (tail - base) % LANES, 1)
        west = pltpu.roll(rim[rim_slots - 1, block], (LANES - RIM - base - RIM) % LANES, 1)
        last = jnp.concatenate(
            [source[:, body:sector], jnp.zeros((plane, LANES - tail), jnp.float32)], axis=1
        )
        last = jnp.where((lane >= tail) & (lane < tail + RIM), east, last)
        last = jnp.where(lane >= LANES - RIM, west, last)
        for t in range(body // LANES):
            target[t] = source[:, t * LANES:(t + 1) * LANES]
        target[body // LANES] = last

    def row_of(ref, j):
        return jnp.concatenate(
            [ref[t, pl.ds(j, levels, rows), :] for t in range(width // LANES)], axis=1
        )

    for r in range(4):
        with_rim(r, rate_rows.at[r])
    for r in range(4):
        for j in range(rows):
            rates[r, depth + j] = row_of(rate_rows.at[r], j)

    def to_neighbours(ref, send, recv):
        to_prev = pltpu.make_async_remote_copy(
            src_ref=ref.at[:, pl.ds(depth, depth)], dst_ref=ref.at[:, pl.ds(depth + rows, depth)],
            send_sem=send.at[0], recv_sem=recv.at[0],
            device_id={"lat": lat - 1}, device_id_type=MESH,
        )
        to_next = pltpu.make_async_remote_copy(
            src_ref=ref.at[:, pl.ds(rows, depth)], dst_ref=ref.at[:, pl.ds(0, depth)],
            send_sem=send.at[1], recv_sem=recv.at[1],
            device_id={"lat": lat + 1}, device_id_type=MESH,
        )

        def start():
            pl.when(has_prev)(to_prev.start)
            pl.when(has_next)(to_next.start)

        def arrive():
            pl.when(has_next)(to_prev.wait_recv)
            pl.when(has_prev)(to_next.wait_recv)

        def sent():
            pl.when(has_prev)(to_prev.wait_send)
            pl.when(has_next)(to_next.wait_send)

        return start, arrive, sent

    rate_start, rate_arrive, rate_sent = to_neighbours(rates, rate_send, rate_recv)
    rate_start()

    @pl.when(jnp.logical_not(polar))
    def _():
        for copy in field_rims:
            copy.wait()
        for f in range(fields):
            with_rim(4 + f, filtered.at[f])

    modes = peers * sector

    @pl.when(polar)
    def _():
        column = lax.broadcasted_iota(jnp.int32, (rows, modes), 1)
        row_index = lax.broadcasted_iota(jnp.int32, (rows, modes), 0)
        number = jnp.where(column <= modes // 2, column, column - modes // 2).astype(jnp.float32)
        limit = jnp.zeros((rows, modes), jnp.float32)
        for j in range(rows):
            limit = jnp.where(row_index == j, cutoff_ref[lat * rows + j].astype(jnp.float32), limit)
        ratio = limit / jnp.maximum(number, 1.0)
        damp_ref[...] = jnp.where(number > limit, ratio * ratio, 1.0)
        for copy in table_copies:
            copy.wait()
        for c in range(chunks):
            own = x_ref[:, c * part:(c + 1) * part].reshape(fields * part, sector)
            spectra[c] = product(own, forward[0, 0:sector], forward[1, 0:sector])
        for c in range(chunks):
            for copy in swaps[c]:
                copy.wait_recv()
            total = spectra[c]
            for d in range(1, peers):
                values = swapped[d - 1, :, c * part:(c + 1) * part].reshape(fields * part, sector)
                start, end = d * sector, (d + 1) * sector
                total = total + product(values, forward[0, start:end], forward[1, start:end])
            damped = total.reshape(fields * part // rows, rows, modes) * damp_ref[...][None]
            result = product(damped.reshape(fields * part, modes), inverse[0], inverse[1])
            for t in range(width // LANES):
                block = result[:, t * LANES:(t + 1) * LANES].reshape(fields, part, LANES)
                filtered[:, t, c * part:(c + 1) * part] = block

    edges = [
        to_neighbours(state.at[s], edge_send.at[s // depth], edge_recv.at[s // depth])
        for s in range(0, SUBSTEPS, depth)
    ]

    def couple(j):
        values = [row_of(filtered.at[g], j) for g in range(fields)]
        for f in range(fields):
            total = None
            for g in range(fields):
                term = jnp.tile(power[g * fields + f], (1, width // LANES)) * values[g]
                total = term if total is None else total + term
            state[0, f, depth + j] = total

    outer = list(range(depth)) + list(range(rows - depth, rows))
    inner = list(range(depth, rows - depth))
    for j in outer:
        couple(j)
    edges[0][0]()
    for j in inner:
        couple(j)

    rate_arrive()
    below_last = jnp.where(has_next, 1.0, 0.0)
    for j in range(1, rows + 2 * depth - 1):
        north = rates[0, j]
        if j == depth + rows - 1:
            north = north * below_last
        south = rates[1, j - 1]
        east = rates[2, j]
        west = pltpu.roll(rates[3, j], 1, 1)
        coefs[0, j] = 1.0 - east - west - north - south
        coefs[1, j] = east
        coefs[2, j] = west
        coefs[3, j] = north
        coefs[4, j] = south

    def advance(s, j):
        rate = [coefs[k, j] for k in range(5)]
        for f in range(fields):
            here = state[s, f, j]
            value = (
                rate[0] * here
                + rate[1] * pltpu.roll(here, width - 1, 1)
                + rate[2] * pltpu.roll(here, 1, 1)
                + rate[3] * state[s, f, j + 1]
                + rate[4] * state[s, f, j - 1]
            )
            state[s + 1, f, j] = value

    def advance_rows(s, start, end):
        if end > start:
            @pl.loop(start, end)
            def _(j):
                advance(s, j)

    for s in range(SUBSTEPS):
        reach = depth - 1 - s % depth
        begin, end = depth - reach, depth + rows + reach
        if s % depth == 0:
            edges[s // depth][1]()
        if (s + 1) % depth == 0 and s + 1 < SUBSTEPS:
            advance_rows(s, depth, 2 * depth)
            advance_rows(s, rows, rows + depth)
            edges[(s + 1) // depth][0]()
            advance_rows(s, 2 * depth, rows)
        else:
            advance_rows(s, begin, end)

    for f in range(fields):
        for j in range(rows):
            value = state[SUBSTEPS, f, depth + j]
            for t in range(width // LANES):
                filtered[f, t, pl.ds(j, levels, rows), :] = value[:, t * LANES:(t + 1) * LANES]
    for t in range(width // LANES):
        end = min(sector, (t + 1) * LANES)
        out_ref[:, :, t * LANES:end] = filtered[:, t, :, 0:end - t * LANES]

    rate_sent()
    for edge in edges:
        edge[2]()

    @pl.when(polar)
    def _():
        for c in range(chunks):
            for copy in swaps[c]:
                copy.wait_send()


def shards(peers, bands, adjoint_in, lat_ahead, lat_behind, lon_ahead, lon_behind, coupling, cutoff):
    fields, levels, rows, sector = adjoint_in.shape
    width = -(-(sector + 2 * RIM) // LANES) * LANES
    circle = sector * peers
    forward, inverse = tables(circle, sector, width)
    plane = rows * levels
    flat = [r.reshape(plane, sector) for r in (lat_ahead, lat_behind, lon_ahead, lon_behind)]
    vmem = pl.BlockSpec(memory_space=pltpu.VMEM)
    hbm = pl.BlockSpec(memory_space=pltpu.HBM)
    smem = pl.BlockSpec(memory_space=pltpu.SMEM)
    rim_slots = 1 if peers == 2 else 2
    packs = -(-(4 + fields) // 4)
    tall = rows + 2 * DEPTH
    rounds = SUBSTEPS // DEPTH

    def body(x, a, b, c, d, *rest):
        kernel(peers, bands, fields, rows, levels, sector, width, x, [a, b, c, d], *rest)

    dma = pltpu.SemaphoreType.DMA
    out = pl.pallas_call(
        body,
        out_shape=jax.ShapeDtypeStruct((fields, plane, sector), jnp.float32),
        in_specs=[hbm] * 5 + [vmem, smem] + [hbm] * 2,
        out_specs=vmem,
        scratch_shapes=[
            pltpu.VMEM((fields, plane, sector), jnp.float32),
            pltpu.VMEM((4, plane, sector), jnp.float32),
            pltpu.VMEM(forward.shape, jnp.bfloat16),
            pltpu.VMEM(inverse.shape, jnp.bfloat16),
            pltpu.VMEM((peers - 1, fields, plane, sector), jnp.float32),
            pltpu.VMEM((2, fields * plane // 2, circle), jnp.float32),
            pltpu.VMEM((fields, width // LANES, plane, LANES), jnp.float32),
            pltpu.VMEM((4, width // LANES, plane, LANES), jnp.float32),
            pltpu.VMEM((packs, plane, LANES), jnp.float32),
            pltpu.VMEM((rim_slots, packs, plane, LANES), jnp.float32),
            pltpu.VMEM((4, tall, levels, width), jnp.float32),
            pltpu.VMEM((5, tall, levels, width), jnp.float32),
            pltpu.VMEM((fields * fields, levels, LANES), jnp.float32),
            pltpu.VMEM((SUBSTEPS + 1, fields, tall, levels, width), jnp.float32),
            pltpu.VMEM((rows, circle), jnp.float32),
            dma((5,)), dma((2,)), dma((2, peers - 1)), dma((2, peers - 1)),
            dma((2, rim_slots)), dma((2, rim_slots)),
            dma((2,)), dma((2,)), dma((rounds, 2)), dma((rounds, 2)),
        ],
        compiler_params=pltpu.CompilerParams(
            collective_id=0, has_side_effects=True, vmem_limit_bytes=VMEM_BYTES
        ),
    )(adjoint_in.reshape(fields, plane, sector), *flat, jnp.transpose(coupling, (1, 0, 2)), cutoff, jnp.asarray(forward), jnp.asarray(inverse))
    return out.reshape(fields, levels, rows, sector)


def solution(mesh):
    placed = (
        P("member", "lev", "lat", "lon"),
        P(("member", "lev"), "lat", "lon"),
        P(("member", "lev"), "lat", "lon"),
        P(("member", "lev"), "lat", "lon"),
        P(("member", "lev"), "lat", "lon"),
        P("lev", None, None),
        P(),
    )
    return jax.shard_map(
        functools.partial(shards, mesh.shape["lon"], mesh.shape["lat"]),
        mesh=mesh,
        in_specs=placed,
        out_specs=P("member", "lev", "lat", "lon"),
        check_vma=False,
    )
```

```python
import functools

import jax
import jax.numpy as jnp
import numpy as np
from jax import lax
from jax.experimental import pallas as pl
from jax.experimental.pallas import tpu as pltpu
from jax.sharding import PartitionSpec as P

SUBSTEPS = 6
ROUNDS = (3, 3)
DEPTH = ROUNDS[0]
STARTS = tuple(sum(ROUNDS[:r]) for r in range(len(ROUNDS)))
RIM = 16
LANES = 128
VMEM_BYTES = 67_000_000
MESH = pl.DeviceIdType.MESH


def split_parts(table):
    high = table.astype(jnp.bfloat16)
    low = (table - high.astype(np.float32)).astype(jnp.bfloat16)
    return np.stack([high, low])


def tables(circle, sector, width):
    column = np.arange(circle)
    middle = circle // 2
    wavenumber = np.where(column <= middle, column, column - middle)
    position = np.arange(circle)
    phase = (position[:, None] * wavenumber[None, :]) % circle
    angle = phase * (2.0 * np.pi / circle)
    weight = np.where((column == 0) | (column == middle), 1.0 / circle, 2.0 / circle)
    basis = np.where((column <= middle)[None, :], np.cos(angle), np.sin(angle))
    basis = (basis * np.sqrt(weight)[None, :]).astype(np.float32)
    lane = np.arange(width)
    target = np.where(lane < sector + RIM, lane, lane - width) % circle
    return split_parts(basis), split_parts(np.ascontiguousarray(basis[target].T))


def halves(values):
    high = values.astype(jnp.bfloat16)
    low = (values - high.astype(jnp.float32)).astype(jnp.bfloat16)
    return high, low


def product(values, high_table, low_table):
    high, low = halves(values)
    dot = functools.partial(jnp.dot, preferred_element_type=jnp.float32)
    return dot(high, high_table) + (dot(high, low_table) + dot(low, high_table))


def kernel(
    peers, bands, fields, rows, levels, sector, width,
    x_hbm, rates_hbm, couple_ref, cutoff_ref, forward_hbm, inverse_hbm, out_ref,
    raw, raw_rim, raw_swap, x_ref, rate_ref, forward, inverse, swapped, spectra, filtered, rate_rows, packed, rim, rates, coefs, power, state, damp_ref,
    raw_send, raw_recv, pass_send, pass_recv, load_sem, table_sem, swap_send, swap_recv, rim_send, rim_recv, rate_send, rate_recv, edge_send, edge_recv,
):
    chunks = 2
    lat = lax.axis_index("lat")
    lon = lax.axis_index("lon")
    quarter = bands // 4
    depth = DEPTH

    def in_polar(band):
        return (band < quarter) | (band >= 3 * quarter)

    polar = in_polar(lat)
    has_prev = lat > 0
    has_next = lat < bands - 1
    prev_polar = has_prev & in_polar(lat - 1)
    next_polar = has_next & in_polar(lat + 1)
    filters = polar | prev_polar | next_polar
    plane = rows * levels
    part = plane // chunks
    tail = sector % LANES
    body = sector - tail

    def lon_id(d):
        return {"lon": lax.rem(lon + d + peers, peers)}

    barrier = pltpu.get_barrier_semaphore()
    for d in range(1, peers):
        pl.semaphore_signal(barrier, inc=1, device_id=lon_id(d), device_id_type=MESH)

    @pl.when(has_prev)
    def _():
        pl.semaphore_signal(barrier, inc=1, device_id={"lat": lat - 1}, device_id_type=MESH)

    @pl.when(has_next)
    def _():
        pl.semaphore_signal(barrier, inc=1, device_id={"lat": lat + 1}, device_id_type=MESH)

    rate_refs = [rate_ref.at[r] for r in range(4)]
    loads = [pltpu.make_async_copy(x_hbm, x_ref, load_sem.at[4])]
    loads += [pltpu.make_async_copy(rates_hbm[r], rate_ref.at[r], load_sem.at[r]) for r in range(4)]
    for copy in loads:
        copy.start()

    table_copies = [
        pltpu.make_async_copy(forward_hbm, forward, table_sem.at[0]),
        pltpu.make_async_copy(inverse_hbm, inverse, table_sem.at[1]),
    ]

    @pl.when(filters)
    def _():
        for copy in table_copies:
            copy.start()

    greeters = peers - 1 + has_prev.astype(jnp.int32) + has_next.astype(jnp.int32)
    pl.semaphore_wait(barrier, greeters)

    swaps = [
        [
            pltpu.make_async_remote_copy(
                src_ref=x_hbm.at[:, pl.ds(c * part, part)],
                dst_ref=swapped.at[d - 1, :, pl.ds(c * part, part)],
                send_sem=swap_send.at[c, d - 1], recv_sem=swap_recv.at[c, d - 1],
                device_id=lon_id(-d), device_id_type=MESH,
            )
            for d in range(1, peers)
        ]
        for c in range(chunks)
    ]

    @pl.when(polar)
    def _():
        for copy in swaps[0]:
            copy.start()

    for copy in loads:
        copy.wait()

    def row_of(ref, j):
        return jnp.concatenate(
            [ref[t, pl.ds(j, levels, rows), :] for t in range(width // LANES)], axis=1
        )

    def raw_copy(side, row):
        source = rows - depth + row if side == 0 else row
        return pltpu.make_async_remote_copy(
            src_ref=raw.at[:, source], dst_ref=raw_rim.at[side, :, row],
            send_sem=raw_send.at[side, row], recv_sem=raw_recv.at[side, row],
            device_id={"lat": lat + 1 if side == 0 else lat - 1}, device_id_type=MESH,
        )

    def pass_copy(side, row, d):
        return pltpu.make_async_remote_copy(
            src_ref=raw_rim.at[side, :, row], dst_ref=raw_swap.at[side, d - 1, :, row],
            send_sem=pass_send.at[side, row, d - 1], recv_sem=pass_recv.at[side, row, d - 1],
            device_id=lon_id(-d), device_id_type=MESH,
        )

    @pl.when(polar)
    def _():
        for f in range(fields):
            for t in range(body // LANES):
                filtered[f, t] = x_ref[f, :, t * LANES:(t + 1) * LANES]
            filtered[f, body // LANES, :, 0:tail] = x_ref[f, :, body:sector]
            for j in sorted({*range(depth), *range(rows - depth, rows)}):
                raw[f, j] = row_of(filtered.at[f], j)[:, 0:sector]

        @pl.when(has_next)
        def _():
            for row in range(depth):
                raw_copy(0, row).start()

        @pl.when(has_prev)
        def _():
            for row in range(depth):
                raw_copy(1, row).start()

    sources = [r for r in rate_refs] + [x_ref.at[f] for f in range(fields)]
    lane = lax.broadcasted_iota(jnp.int32, (plane, LANES), 1)
    for block in range(packed.shape[0]):
        value = jnp.zeros((plane, LANES), jnp.float32)
        for k, source in enumerate(sources[4 * block:4 * block + 4]):
            first = source[:, 0:LANES]
            last = jnp.concatenate(
                [source[:, body:sector], jnp.zeros((plane, LANES - tail), jnp.float32)], axis=1
            )
            base = 32 * k
            if base:
                first = pltpu.roll(first, base, 1)
            last = pltpu.roll(last, (base + RIM - (tail - RIM)) % LANES, 1)
            value = jnp.where((lane >= base) & (lane < base + RIM), first, value)
            value = jnp.where((lane >= base + RIM) & (lane < base + 2 * RIM), last, value)
        packed[block] = value

    rim_slots = rim.shape[0]

    def rim_copies(stage, start, stop):
        return [
            pltpu.make_async_remote_copy(
                src_ref=packed.at[start:stop], dst_ref=rim.at[slot, start:stop],
                send_sem=rim_send.at[stage, slot], recv_sem=rim_recv.at[stage, slot],
                device_id=lon_id(-1 if slot == 0 else 1), device_id_type=MESH,
            )
            for slot in range(rim_slots)
        ]

    rate_rims, field_rims = rim_copies(0, 0, 1), rim_copies(1, 1, packed.shape[0])
    for copy in rate_rims:
        copy.start()

    @pl.when(polar)
    def _():
        for c in range(1, chunks):
            for copy in swaps[c]:
                copy.start()

    @pl.when(jnp.logical_not(polar))
    def _():
        for copy in field_rims:
            copy.start()

    def entry(g, f):
        value = jnp.broadcast_to(couple_ref[g, :, f:f + 1], (levels, LANES))
        return value + 1.0 if g == f else value

    once = [[entry(g, f) for f in range(fields)] for g in range(fields)]

    def multiply(a, b):
        return [
            [sum(a[g][h] * b[h][f] for h in range(fields)) for f in range(fields)]
            for g in range(fields)
        ]

    result = once
    for _ in range(SUBSTEPS - 1):
        result = multiply(result, once)
    for g in range(fields):
        for f in range(fields):
            power[g * fields + f] = result[g][f]

    @pl.when(jnp.logical_not(has_prev))
    def _():
        rates[:, 0:depth] = jnp.zeros((4, depth, levels, width), jnp.float32)
        for s in STARTS:
            state[s, :, 0:depth] = jnp.zeros((fields, depth, levels, width), jnp.float32)

    @pl.when(jnp.logical_not(has_next))
    def _():
        rates[:, depth + rows:] = jnp.zeros((4, depth, levels, width), jnp.float32)
        for s in STARTS:
            state[s, :, depth + rows:] = jnp.zeros((fields, depth, levels, width), jnp.float32)

    for copy in rate_rims:
        copy.wait()

    def with_rim(index, target):
        source = sources[index]
        block, base = index // 4, 32 * (index % 4)
        east = pltpu.roll(rim[0, block], (tail - base) % LANES, 1)
        west = pltpu.roll(rim[rim_slots - 1, block], (LANES - RIM - base - RIM) % LANES, 1)
        last = jnp.concatenate(
            [source[:, body:sector], jnp.zeros((plane, LANES - tail), jnp.float32)], axis=1
        )
        last = jnp.where((lane >= tail) & (lane < tail + RIM), east, last)
        last = jnp.where(lane >= LANES - RIM, west, last)
        for t in range(body // LANES):
            target[t] = source[:, t * LANES:(t + 1) * LANES]
        target[body // LANES] = last

    for r in range(4):
        with_rim(r, rate_rows.at[r])
    for r in range(4):
        for j in range(rows):
            rates[r, depth + j] = row_of(rate_rows.at[r], j)

    def to_neighbours(ref, reach, send, recv, prev_gives=True, self_gives=True, next_gives=True):
        to_prev = pltpu.make_async_remote_copy(
            src_ref=ref.at[:, pl.ds(depth, reach)], dst_ref=ref.at[:, pl.ds(depth + rows, reach)],
            send_sem=send.at[0], recv_sem=recv.at[0],
            device_id={"lat": lat - 1}, device_id_type=MESH,
        )
        to_next = pltpu.make_async_remote_copy(
            src_ref=ref.at[:, pl.ds(depth + rows - reach, reach)], dst_ref=ref.at[:, pl.ds(depth - reach, reach)],
            send_sem=send.at[1], recv_sem=recv.at[1],
            device_id={"lat": lat + 1}, device_id_type=MESH,
        )

        def start():
            pl.when(has_prev & self_gives)(to_prev.start)
            pl.when(has_next & self_gives)(to_next.start)

        def arrive():
            pl.when(has_next & next_gives)(to_prev.wait_recv)
            pl.when(has_prev & prev_gives)(to_next.wait_recv)

        def sent():
            pl.when(has_prev & self_gives)(to_prev.wait_send)
            pl.when(has_next & self_gives)(to_next.wait_send)

        return start, arrive, sent

    rate_start, rate_arrive, rate_sent = to_neighbours(rates, depth, rate_send, rate_recv)
    rate_start()

    edges = []
    for r, reach in enumerate(ROUNDS):
        gives = (True, True, True)
        if r == 0:
            gives = tuple(jnp.logical_not(p) for p in (prev_polar, polar, next_polar))
        edges.append(to_neighbours(state.at[STARTS[r]], reach, edge_send.at[r], edge_recv.at[r], *gives))

    def mix(values, target):
        for f in range(fields):
            total = None
            for g in range(fields):
                term = jnp.tile(power[g * fields + f], (1, width // LANES)) * values[g]
                total = term if total is None else total + term
            state[0, f, target] = total

    def couple(j):
        mix([row_of(filtered.at[g], j) for g in range(fields)], depth + j)

    outer = sorted({*range(depth), *range(rows - depth, rows)})
    inner = [j for j in range(rows) if j not in outer]

    @pl.when(jnp.logical_not(polar))
    def _():
        for copy in field_rims:
            copy.wait()
        for f in range(fields):
            with_rim(4 + f, filtered.at[f])
        for j in outer:
            couple(j)
        edges[0][0]()
        for j in inner:
            couple(j)

    sides = ((0, prev_polar), (1, next_polar))
    for side, present in sides:
        @pl.when(present)
        def _():
            for row in range(depth):
                raw_copy(side, row).wait_recv()
                for d in range(1, peers):
                    pass_copy(side, row, d).start()

    modes = peers * sector

    def damping(shape, limit):
        column = lax.broadcasted_iota(jnp.int32, shape, 1)
        number = jnp.where(column <= modes // 2, column, column - modes // 2).astype(jnp.float32)
        ratio = limit / jnp.maximum(number, 1.0)
        return jnp.where(number > limit, ratio * ratio, 1.0)

    @pl.when(filters)
    def _():
        for copy in table_copies:
            copy.wait()

    @pl.when(polar)
    def _():
        row_index = lax.broadcasted_iota(jnp.int32, (rows, modes), 0)
        limit = jnp.zeros((rows, modes), jnp.float32)
        for j in range(rows):
            limit = jnp.where(row_index == j, cutoff_ref[lat * rows + j].astype(jnp.float32), limit)
        damp_ref[...] = damping((rows, modes), limit)
        for c in range(chunks):
            own = x_ref[:, c * part:(c + 1) * part].reshape(fields * part, sector)
            spectra[c] = product(own, forward[0, 0:sector], forward[1, 0:sector])

    rate_arrive()
    below_last = jnp.where(has_next, 1.0, 0.0)
    for j in range(1, rows + 2 * depth - 1):
        north = rates[0, j]
        if j == depth + rows - 1:
            north = north * below_last
        south = rates[1, j - 1]
        east = rates[2, j]
        west = pltpu.roll(rates[3, j], 1, 1)
        coefs[0, j] = 1.0 - east - west - north - south
        coefs[1, j] = east
        coefs[2, j] = west
        coefs[3, j] = north
        coefs[4, j] = south

    @pl.when(polar)
    def _():
        for c in range(chunks):
            for copy in swaps[c]:
                copy.wait_recv()
            total = spectra[c]
            for d in range(1, peers):
                values = swapped[d - 1, :, c * part:(c + 1) * part].reshape(fields * part, sector)
                start, end = d * sector, (d + 1) * sector
                total = total + product(values, forward[0, start:end], forward[1, start:end])
            damped = total.reshape(fields * part // rows, rows, modes) * damp_ref[...][None]
            result = product(damped.reshape(fields * part, modes), inverse[0], inverse[1])
            for t in range(width // LANES):
                block = result[:, t * LANES:(t + 1) * LANES].reshape(fields, part, LANES)
                filtered[:, t, c * part:(c + 1) * part] = block
        for j in range(rows):
            couple(j)

    for side, present in sides:
        @pl.when(present)
        def _():
            count = fields * depth * levels
            total = product(raw_rim[side].reshape(count, sector), forward[0, 0:sector], forward[1, 0:sector])
            for d in range(1, peers):
                for row in range(depth):
                    pass_copy(side, row, d).wait_recv()
                start, end = d * sector, (d + 1) * sector
                total = total + product(
                    raw_swap[side, d - 1].reshape(count, sector), forward[0, start:end], forward[1, start:end]
                )
            begin = lat * rows - depth if side == 0 else (lat + 1) * rows
            limits = [cutoff_ref[begin + row].astype(jnp.float32) for row in range(depth)]
            table = jnp.stack([damping((levels, modes), limit) for limit in limits])
            damped = total.reshape(fields, depth, levels, modes) * table[None]
            result = product(damped.reshape(count, modes), inverse[0], inverse[1])
            result = result.reshape(fields, depth, levels, width)
            for row in range(depth):
                mix([result[g, row] for g in range(fields)], row if side == 0 else depth + rows + row)

    def advance(s, j):
        rate = [coefs[k, j] for k in range(5)]
        for f in range(fields):
            here = state[s, f, j]
            value = (
                rate[0] * here
                + rate[1] * pltpu.roll(here, width - 1, 1)
                + rate[2] * pltpu.roll(here, 1, 1)
                + rate[3] * state[s, f, j + 1]
                + rate[4] * state[s, f, j - 1]
            )
            state[s + 1, f, j] = value

    def advance_rows(s, start, end):
        if end > start:
            @pl.loop(start, end)
            def _(j):
                advance(s, j)

    for r, first in enumerate(STARTS):
        edges[r][1]()
        for k in range(ROUNDS[r]):
            s = first + k
            reach = ROUNDS[r] - 1 - k
            if reach == 0 and s + 1 < SUBSTEPS:
                ahead = ROUNDS[r + 1]
                advance_rows(s, depth, depth + ahead)
                advance_rows(s, depth + rows - ahead, depth + rows)
                edges[r + 1][0]()
                advance_rows(s, depth + ahead, depth + rows - ahead)
            else:
                advance_rows(s, depth - reach, depth + rows + reach)

    for f in range(fields):
        for j in range(rows):
            value = state[SUBSTEPS, f, depth + j]
            for t in range(width // LANES):
                filtered[f, t, pl.ds(j, levels, rows), :] = value[:, t * LANES:(t + 1) * LANES]
    for t in range(width // LANES):
        end = min(sector, (t + 1) * LANES)
        out_ref[:, :, t * LANES:end] = filtered[:, t, :, 0:end - t * LANES]

    rate_sent()
    for edge in edges:
        edge[2]()

    @pl.when(polar)
    def _():
        for c in range(chunks):
            for copy in swaps[c]:
                copy.wait_send()

        @pl.when(has_next)
        def _():
            for row in range(depth):
                raw_copy(0, row).wait_send()

        @pl.when(has_prev)
        def _():
            for row in range(depth):
                raw_copy(1, row).wait_send()

    for side, present in sides:
        @pl.when(present)
        def _():
            for row in range(depth):
                for d in range(1, peers):
                    pass_copy(side, row, d).wait_send()


def shards(peers, bands, adjoint_in, lat_ahead, lat_behind, lon_ahead, lon_behind, coupling, cutoff):
    fields, levels, rows, sector = adjoint_in.shape
    width = -(-(sector + 2 * RIM) // LANES) * LANES
    circle = sector * peers
    forward, inverse = tables(circle, sector, width)
    plane = rows * levels
    flat = [r.reshape(plane, sector) for r in (lat_ahead, lat_behind, lon_ahead, lon_behind)]
    vmem = pl.BlockSpec(memory_space=pltpu.VMEM)
    hbm = pl.BlockSpec(memory_space=pltpu.HBM)
    smem = pl.BlockSpec(memory_space=pltpu.SMEM)
    rim_slots = 1 if peers == 2 else 2
    packs = -(-(4 + fields) // 4)
    tall = rows + 2 * DEPTH
    rounds = len(ROUNDS)

    def body(x, a, b, c, d, *rest):
        kernel(peers, bands, fields, rows, levels, sector, width, x, [a, b, c, d], *rest)

    dma = pltpu.SemaphoreType.DMA
    out = pl.pallas_call(
        body,
        out_shape=jax.ShapeDtypeStruct((fields, plane, sector), jnp.float32),
        in_specs=[hbm] * 5 + [vmem, smem] + [hbm] * 2,
        out_specs=vmem,
        scratch_shapes=[
            pltpu.VMEM((fields, rows, levels, sector), jnp.float32),
            pltpu.VMEM((2, fields, DEPTH, levels, sector), jnp.float32),
            pltpu.VMEM((2, peers - 1, fields, DEPTH, levels, sector), jnp.float32),
            pltpu.VMEM((fields, plane, sector), jnp.float32),
            pltpu.VMEM((4, plane, sector), jnp.float32),
            pltpu.VMEM(forward.shape, jnp.bfloat16),
            pltpu.VMEM(inverse.shape, jnp.bfloat16),
            pltpu.VMEM((peers - 1, fields, plane, sector), jnp.float32),
            pltpu.VMEM((2, fields * plane // 2, circle), jnp.float32),
            pltpu.VMEM((fields, width // LANES, plane, LANES), jnp.float32),
            pltpu.VMEM((4, width // LANES, plane, LANES), jnp.float32),
            pltpu.VMEM((packs, plane, LANES), jnp.float32),
            pltpu.VMEM((rim_slots, packs, plane, LANES), jnp.float32),
            pltpu.VMEM((4, tall, levels, width), jnp.float32),
            pltpu.VMEM((5, tall, levels, width), jnp.float32),
            pltpu.VMEM((fields * fields, levels, LANES), jnp.float32),
            pltpu.VMEM((SUBSTEPS + 1, fields, tall, levels, width), jnp.float32),
            pltpu.VMEM((rows, circle), jnp.float32),
            dma((2, DEPTH)), dma((2, DEPTH)), dma((2, DEPTH, peers - 1)), dma((2, DEPTH, peers - 1)),
            dma((5,)), dma((2,)), dma((2, peers - 1)), dma((2, peers - 1)),
            dma((2, rim_slots)), dma((2, rim_slots)),
            dma((2,)), dma((2,)), dma((rounds, 2)), dma((rounds, 2)),
        ],
        compiler_params=pltpu.CompilerParams(
            collective_id=0, has_side_effects=True, vmem_limit_bytes=VMEM_BYTES
        ),
    )(adjoint_in.reshape(fields, plane, sector), *flat, jnp.transpose(coupling, (1, 0, 2)), cutoff, jnp.asarray(forward), jnp.asarray(inverse))
    return out.reshape(fields, levels, rows, sector)


def solution(mesh):
    placed = (
        P("member", "lev", "lat", "lon"),
        P(("member", "lev"), "lat", "lon"),
        P(("member", "lev"), "lat", "lon"),
        P(("member", "lev"), "lat", "lon"),
        P(("member", "lev"), "lat", "lon"),
        P("lev", None, None),
        P(),
    )
    return jax.shard_map(
        functools.partial(shards, mesh.shape["lon"], mesh.shape["lat"]),
        mesh=mesh,
        in_specs=placed,
        out_specs=P("member", "lev", "lat", "lon"),
        check_vma=False,
    )
```

```python
import functools

import jax
import jax.numpy as jnp
import numpy as np
from jax import lax
from jax.experimental import pallas as pl
from jax.experimental.pallas import tpu as pltpu
from jax.sharding import PartitionSpec as P

SUBSTEPS = 6
ROUNDS = (4, 2)
DEPTH = ROUNDS[0]
STARTS = tuple(sum(ROUNDS[:r]) for r in range(len(ROUNDS)))
RIM = 16
LANES = 128
VMEM_BYTES = 66_200_000
MESH = pl.DeviceIdType.MESH


def split_parts(table):
    high = table.astype(jnp.bfloat16)
    low = (table - high.astype(np.float32)).astype(jnp.bfloat16)
    return np.stack([high, low])


def tables(circle, sector, width):
    column = np.arange(circle)
    middle = circle // 2
    wavenumber = np.where(column <= middle, column, column - middle)
    position = np.arange(circle)
    phase = (position[:, None] * wavenumber[None, :]) % circle
    angle = phase * (2.0 * np.pi / circle)
    weight = np.where((column == 0) | (column == middle), 1.0 / circle, 2.0 / circle)
    basis = np.where((column <= middle)[None, :], np.cos(angle), np.sin(angle))
    basis = (basis * np.sqrt(weight)[None, :]).astype(np.float32)
    lane = np.arange(width)
    target = np.where(lane < sector + RIM, lane, lane - width) % circle
    return split_parts(basis), split_parts(np.ascontiguousarray(basis[target].T))


def halves(values):
    high = values.astype(jnp.bfloat16)
    low = (values - high.astype(jnp.float32)).astype(jnp.bfloat16)
    return high, low


def product(values, high_table, low_table):
    high, low = halves(values)
    dot = functools.partial(jnp.dot, preferred_element_type=jnp.float32)
    return dot(high, high_table) + (dot(high, low_table) + dot(low, high_table))


def kernel(
    peers, bands, fields, rows, levels, sector, width,
    x_hbm, rates_hbm, couple_ref, cutoff_ref, forward_hbm, inverse_hbm, out_ref,
    raw, raw_rim, raw_swap, x_ref, rate_ref, forward, inverse, swapped, spectra, filtered, rate_rows, packed, rim, rates, coefs, power, state, damp_ref,
    raw_send, raw_recv, pass_send, pass_recv, load_sem, table_sem, swap_send, swap_recv, rim_send, rim_recv, rate_send, rate_recv, edge_send, edge_recv,
):
    chunks = 2
    lat = lax.axis_index("lat")
    lon = lax.axis_index("lon")
    quarter = bands // 4
    depth = DEPTH

    def in_polar(band):
        return (band < quarter) | (band >= 3 * quarter)

    polar = in_polar(lat)
    has_prev = lat > 0
    has_next = lat < bands - 1
    prev_polar = has_prev & in_polar(lat - 1)
    next_polar = has_next & in_polar(lat + 1)
    filters = polar | prev_polar | next_polar
    plane = rows * levels
    part = plane // chunks
    tail = sector % LANES
    body = sector - tail

    def lon_id(d):
        return {"lon": lax.rem(lon + d + peers, peers)}

    barrier = pltpu.get_barrier_semaphore()
    for d in range(1, peers):
        pl.semaphore_signal(barrier, inc=1, device_id=lon_id(d), device_id_type=MESH)

    @pl.when(has_prev)
    def _():
        pl.semaphore_signal(barrier, inc=1, device_id={"lat": lat - 1}, device_id_type=MESH)

    @pl.when(has_next)
    def _():
        pl.semaphore_signal(barrier, inc=1, device_id={"lat": lat + 1}, device_id_type=MESH)

    rate_refs = [rate_ref.at[r] for r in range(4)]
    loads = [pltpu.make_async_copy(x_hbm, x_ref, load_sem.at[4])]
    loads += [pltpu.make_async_copy(rates_hbm[r], rate_ref.at[r], load_sem.at[r]) for r in range(4)]
    for copy in loads:
        copy.start()

    table_copies = [
        pltpu.make_async_copy(forward_hbm, forward, table_sem.at[0]),
        pltpu.make_async_copy(inverse_hbm, inverse, table_sem.at[1]),
    ]

    @pl.when(filters)
    def _():
        for copy in table_copies:
            copy.start()

    greeters = peers - 1 + has_prev.astype(jnp.int32) + has_next.astype(jnp.int32)
    pl.semaphore_wait(barrier, greeters)

    swaps = [
        [
            pltpu.make_async_remote_copy(
                src_ref=x_hbm.at[:, pl.ds(c * part, part)],
                dst_ref=swapped.at[d - 1, :, pl.ds(c * part, part)],
                send_sem=swap_send.at[c, d - 1], recv_sem=swap_recv.at[c, d - 1],
                device_id=lon_id(-d), device_id_type=MESH,
            )
            for d in range(1, peers)
        ]
        for c in range(chunks)
    ]

    @pl.when(polar)
    def _():
        for copy in swaps[0]:
            copy.start()

    for copy in loads:
        copy.wait()

    def row_of(ref, j):
        return jnp.concatenate(
            [ref[t, pl.ds(j, levels, rows), :] for t in range(width // LANES)], axis=1
        )

    def raw_copy(side, row):
        source = rows - depth + row if side == 0 else row
        return pltpu.make_async_remote_copy(
            src_ref=raw.at[:, source], dst_ref=raw_rim.at[side, :, row],
            send_sem=raw_send.at[side, row], recv_sem=raw_recv.at[side, row],
            device_id={"lat": lat + 1 if side == 0 else lat - 1}, device_id_type=MESH,
        )

    def pass_copy(side, row, d):
        return pltpu.make_async_remote_copy(
            src_ref=raw_rim.at[side, :, row], dst_ref=raw_swap.at[side, d - 1, :, row],
            send_sem=pass_send.at[side, row, d - 1], recv_sem=pass_recv.at[side, row, d - 1],
            device_id=lon_id(-d), device_id_type=MESH,
        )

    @pl.when(polar)
    def _():
        for f in range(fields):
            for t in range(body // LANES):
                filtered[f, t] = x_ref[f, :, t * LANES:(t + 1) * LANES]
            filtered[f, body // LANES, :, 0:tail] = x_ref[f, :, body:sector]
            for j in sorted({*range(depth), *range(rows - depth, rows)}):
                raw[f, j] = row_of(filtered.at[f], j)[:, 0:sector]

        @pl.when(has_next)
        def _():
            for row in range(depth):
                raw_copy(0, row).start()

        @pl.when(has_prev)
        def _():
            for row in range(depth):
                raw_copy(1, row).start()

    sources = [r for r in rate_refs] + [x_ref.at[f] for f in range(fields)]
    lane = lax.broadcasted_iota(jnp.int32, (plane, LANES), 1)
    for block in range(packed.shape[0]):
        value = jnp.zeros((plane, LANES), jnp.float32)
        for k, source in enumerate(sources[4 * block:4 * block + 4]):
            first = source[:, 0:LANES]
            last = jnp.concatenate(
                [source[:, body:sector], jnp.zeros((plane, LANES - tail), jnp.float32)], axis=1
            )
            base = 32 * k
            if base:
                first = pltpu.roll(first, base, 1)
            last = pltpu.roll(last, (base + RIM - (tail - RIM)) % LANES, 1)
            value = jnp.where((lane >= base) & (lane < base + RIM), first, value)
            value = jnp.where((lane >= base + RIM) & (lane < base + 2 * RIM), last, value)
        packed[block] = value

    rim_slots = rim.shape[0]

    def rim_copies(stage, start, stop):
        return [
            pltpu.make_async_remote_copy(
                src_ref=packed.at[start:stop], dst_ref=rim.at[slot, start:stop],
                send_sem=rim_send.at[stage, slot], recv_sem=rim_recv.at[stage, slot],
                device_id=lon_id(-1 if slot == 0 else 1), device_id_type=MESH,
            )
            for slot in range(rim_slots)
        ]

    rate_rims, field_rims = rim_copies(0, 0, 1), rim_copies(1, 1, packed.shape[0])
    for copy in rate_rims:
        copy.start()

    @pl.when(polar)
    def _():
        for c in range(1, chunks):
            for copy in swaps[c]:
                copy.start()

    @pl.when(jnp.logical_not(polar))
    def _():
        for copy in field_rims:
            copy.start()

    def entry(g, f):
        value = jnp.broadcast_to(couple_ref[g, :, f:f + 1], (levels, LANES))
        return value + 1.0 if g == f else value

    once = [[entry(g, f) for f in range(fields)] for g in range(fields)]

    def multiply(a, b):
        return [
            [sum(a[g][h] * b[h][f] for h in range(fields)) for f in range(fields)]
            for g in range(fields)
        ]

    result = once
    for _ in range(SUBSTEPS - 1):
        result = multiply(result, once)
    for g in range(fields):
        for f in range(fields):
            power[g * fields + f] = result[g][f]

    @pl.when(jnp.logical_not(has_prev))
    def _():
        rates[:, 0:depth] = jnp.zeros((4, depth, levels, width), jnp.float32)
        for s in STARTS:
            state[s, :, 0:depth] = jnp.zeros((fields, depth, levels, width), jnp.float32)

    @pl.when(jnp.logical_not(has_next))
    def _():
        rates[:, depth + rows:] = jnp.zeros((4, depth, levels, width), jnp.float32)
        for s in STARTS:
            state[s, :, depth + rows:] = jnp.zeros((fields, depth, levels, width), jnp.float32)

    for copy in rate_rims:
        copy.wait()

    def with_rim(index, target):
        source = sources[index]
        block, base = index // 4, 32 * (index % 4)
        east = pltpu.roll(rim[0, block], (tail - base) % LANES, 1)
        west = pltpu.roll(rim[rim_slots - 1, block], (LANES - RIM - base - RIM) % LANES, 1)
        last = jnp.concatenate(
            [source[:, body:sector], jnp.zeros((plane, LANES - tail), jnp.float32)], axis=1
        )
        last = jnp.where((lane >= tail) & (lane < tail + RIM), east, last)
        last = jnp.where(lane >= LANES - RIM, west, last)
        for t in range(body // LANES):
            target[t] = source[:, t * LANES:(t + 1) * LANES]
        target[body // LANES] = last

    for r in range(4):
        with_rim(r, rate_rows.at[r])
    for r in range(4):
        for j in range(rows):
            rates[r, depth + j] = row_of(rate_rows.at[r], j)

    def to_neighbours(ref, reach, send, recv, prev_gives=True, self_gives=True, next_gives=True):
        to_prev = pltpu.make_async_remote_copy(
            src_ref=ref.at[:, pl.ds(depth, reach)], dst_ref=ref.at[:, pl.ds(depth + rows, reach)],
            send_sem=send.at[0], recv_sem=recv.at[0],
            device_id={"lat": lat - 1}, device_id_type=MESH,
        )
        to_next = pltpu.make_async_remote_copy(
            src_ref=ref.at[:, pl.ds(depth + rows - reach, reach)], dst_ref=ref.at[:, pl.ds(depth - reach, reach)],
            send_sem=send.at[1], recv_sem=recv.at[1],
            device_id={"lat": lat + 1}, device_id_type=MESH,
        )

        def start():
            pl.when(has_prev & self_gives)(to_prev.start)
            pl.when(has_next & self_gives)(to_next.start)

        def arrive():
            pl.when(has_next & next_gives)(to_prev.wait_recv)
            pl.when(has_prev & prev_gives)(to_next.wait_recv)

        def sent():
            pl.when(has_prev & self_gives)(to_prev.wait_send)
            pl.when(has_next & self_gives)(to_next.wait_send)

        return start, arrive, sent

    rate_start, rate_arrive, rate_sent = to_neighbours(rates, depth - 1, rate_send, rate_recv)
    behind = pltpu.make_async_remote_copy(
        src_ref=rates.at[1, rows], dst_ref=rates.at[1, 0],
        send_sem=rate_send.at[2], recv_sem=rate_recv.at[2],
        device_id={"lat": lat + 1}, device_id_type=MESH,
    )
    rate_start()
    pl.when(has_next)(behind.start)

    edges = []
    for r, reach in enumerate(ROUNDS):
        gives = (True, True, True)
        if r == 0:
            gives = tuple(jnp.logical_not(p) for p in (prev_polar, polar, next_polar))
        edges.append(to_neighbours(state.at[STARTS[r]], reach, edge_send.at[r], edge_recv.at[r], *gives))

    def mix(values, target):
        for f in range(fields):
            total = None
            for g in range(fields):
                term = jnp.tile(power[g * fields + f], (1, width // LANES)) * values[g]
                total = term if total is None else total + term
            state[0, f, target] = total

    def couple(j):
        mix([row_of(filtered.at[g], j) for g in range(fields)], depth + j)

    outer = sorted({*range(depth), *range(rows - depth, rows)})
    inner = [j for j in range(rows) if j not in outer]

    @pl.when(jnp.logical_not(polar))
    def _():
        for copy in field_rims:
            copy.wait()
        for f in range(fields):
            with_rim(4 + f, filtered.at[f])
        for j in outer:
            couple(j)
        edges[0][0]()
        for j in inner:
            couple(j)

    sides = ((0, prev_polar), (1, next_polar))
    for side, present in sides:
        @pl.when(present)
        def _():
            for row in range(depth):
                raw_copy(side, row).wait_recv()
                for d in range(1, peers):
                    pass_copy(side, row, d).start()

    modes = peers * sector

    def damping(shape, limit):
        column = lax.broadcasted_iota(jnp.int32, shape, 1)
        number = jnp.where(column <= modes // 2, column, column - modes // 2).astype(jnp.float32)
        ratio = limit / jnp.maximum(number, 1.0)
        return jnp.where(number > limit, ratio * ratio, 1.0)

    @pl.when(filters)
    def _():
        for copy in table_copies:
            copy.wait()

    @pl.when(polar)
    def _():
        row_index = lax.broadcasted_iota(jnp.int32, (rows, modes), 0)
        limit = jnp.zeros((rows, modes), jnp.float32)
        for j in range(rows):
            limit = jnp.where(row_index == j, cutoff_ref[lat * rows + j].astype(jnp.float32), limit)
        damp_ref[...] = damping((rows, modes), limit)
        for c in range(chunks):
            own = x_ref[:, c * part:(c + 1) * part].reshape(fields * part, sector)
            spectra[c] = product(own, forward[0, 0:sector], forward[1, 0:sector])

    rate_arrive()
    pl.when(has_prev)(behind.wait_recv)
    below_last = jnp.where(has_next, 1.0, 0.0)
    for j in range(1, rows + 2 * depth - 1):
        north = rates[0, j]
        if j == depth + rows - 1:
            north = north * below_last
        south = rates[1, j - 1]
        east = rates[2, j]
        west = pltpu.roll(rates[3, j], 1, 1)
        coefs[0, j] = 1.0 - east - west - north - south
        coefs[1, j] = east
        coefs[2, j] = west
        coefs[3, j] = north
        coefs[4, j] = south

    @pl.when(polar)
    def _():
        for c in range(chunks):
            for copy in swaps[c]:
                copy.wait_recv()
            total = spectra[c]
            for d in range(1, peers):
                values = swapped[d - 1, :, c * part:(c + 1) * part].reshape(fields * part, sector)
                start, end = d * sector, (d + 1) * sector
                total = total + product(values, forward[0, start:end], forward[1, start:end])
            damped = total.reshape(fields * part // rows, rows, modes) * damp_ref[...][None]
            result = product(damped.reshape(fields * part, modes), inverse[0], inverse[1])
            for t in range(width // LANES):
                block = result[:, t * LANES:(t + 1) * LANES].reshape(fields, part, LANES)
                filtered[:, t, c * part:(c + 1) * part] = block
        for j in range(rows):
            couple(j)

    for side, present in sides:
        @pl.when(present)
        def _():
            count = fields * depth * levels
            total = product(raw_rim[side].reshape(count, sector), forward[0, 0:sector], forward[1, 0:sector])
            for d in range(1, peers):
                for row in range(depth):
                    pass_copy(side, row, d).wait_recv()
                start, end = d * sector, (d + 1) * sector
                total = total + product(
                    raw_swap[side, d - 1].reshape(count, sector), forward[0, start:end], forward[1, start:end]
                )
            begin = lat * rows - depth if side == 0 else (lat + 1) * rows
            limits = [cutoff_ref[begin + row].astype(jnp.float32) for row in range(depth)]
            table = jnp.stack([damping((levels, modes), limit) for limit in limits])
            damped = total.reshape(fields, depth, levels, modes) * table[None]
            result = product(damped.reshape(count, modes), inverse[0], inverse[1])
            result = result.reshape(fields, depth, levels, width)
            for row in range(depth):
                mix([result[g, row] for g in range(fields)], row if side == 0 else depth + rows + row)

    def advance(s, j):
        rate = [coefs[k, j] for k in range(5)]
        for f in range(fields):
            here = state[s, f, j]
            value = (
                rate[0] * here
                + rate[1] * pltpu.roll(here, width - 1, 1)
                + rate[2] * pltpu.roll(here, 1, 1)
                + rate[3] * state[s, f, j + 1]
                + rate[4] * state[s, f, j - 1]
            )
            state[s + 1, f, j] = value

    def advance_rows(s, start, end):
        if end > start:
            @pl.loop(start, end)
            def _(j):
                advance(s, j)

    for r, first in enumerate(STARTS):
        edges[r][1]()
        for k in range(ROUNDS[r]):
            s = first + k
            reach = ROUNDS[r] - 1 - k
            if reach == 0 and s + 1 < SUBSTEPS:
                ahead = ROUNDS[r + 1]
                advance_rows(s, depth, depth + ahead)
                advance_rows(s, depth + rows - ahead, depth + rows)
                edges[r + 1][0]()
                advance_rows(s, depth + ahead, depth + rows - ahead)
            else:
                advance_rows(s, depth - reach, depth + rows + reach)

    for f in range(fields):
        for j in range(rows):
            value = state[SUBSTEPS, f, depth + j]
            for t in range(width // LANES):
                filtered[f, t, pl.ds(j, levels, rows), :] = value[:, t * LANES:(t + 1) * LANES]
    for t in range(width // LANES):
        end = min(sector, (t + 1) * LANES)
        out_ref[:, :, t * LANES:end] = filtered[:, t, :, 0:end - t * LANES]

    rate_sent()
    pl.when(has_next)(behind.wait_send)
    for edge in edges:
        edge[2]()

    @pl.when(polar)
    def _():
        for c in range(chunks):
            for copy in swaps[c]:
                copy.wait_send()

        @pl.when(has_next)
        def _():
            for row in range(depth):
                raw_copy(0, row).wait_send()

        @pl.when(has_prev)
        def _():
            for row in range(depth):
                raw_copy(1, row).wait_send()

    for side, present in sides:
        @pl.when(present)
        def _():
            for row in range(depth):
                for d in range(1, peers):
                    pass_copy(side, row, d).wait_send()


def shards(peers, bands, adjoint_in, lat_ahead, lat_behind, lon_ahead, lon_behind, coupling, cutoff):
    fields, levels, rows, sector = adjoint_in.shape
    width = -(-(sector + 2 * RIM) // LANES) * LANES
    circle = sector * peers
    forward, inverse = tables(circle, sector, width)
    plane = rows * levels
    flat = [r.reshape(plane, sector) for r in (lat_ahead, lat_behind, lon_ahead, lon_behind)]
    vmem = pl.BlockSpec(memory_space=pltpu.VMEM)
    hbm = pl.BlockSpec(memory_space=pltpu.HBM)
    smem = pl.BlockSpec(memory_space=pltpu.SMEM)
    rim_slots = 1 if peers == 2 else 2
    packs = -(-(4 + fields) // 4)
    tall = rows + 2 * DEPTH
    rounds = len(ROUNDS)

    def body(x, a, b, c, d, *rest):
        kernel(peers, bands, fields, rows, levels, sector, width, x, [a, b, c, d], *rest)

    dma = pltpu.SemaphoreType.DMA
    out = pl.pallas_call(
        body,
        out_shape=jax.ShapeDtypeStruct((fields, plane, sector), jnp.float32),
        in_specs=[hbm] * 5 + [vmem, smem] + [hbm] * 2,
        out_specs=vmem,
        scratch_shapes=[
            pltpu.VMEM((fields, rows, levels, sector), jnp.float32),
            pltpu.VMEM((2, fields, DEPTH, levels, sector), jnp.float32),
            pltpu.VMEM((2, peers - 1, fields, DEPTH, levels, sector), jnp.float32),
            pltpu.VMEM((fields, plane, sector), jnp.float32),
            pltpu.VMEM((4, plane, sector), jnp.float32),
            pltpu.VMEM(forward.shape, jnp.bfloat16),
            pltpu.VMEM(inverse.shape, jnp.bfloat16),
            pltpu.VMEM((peers - 1, fields, plane, sector), jnp.float32),
            pltpu.VMEM((2, fields * plane // 2, circle), jnp.float32),
            pltpu.VMEM((fields, width // LANES, plane, LANES), jnp.float32),
            pltpu.VMEM((4, width // LANES, plane, LANES), jnp.float32),
            pltpu.VMEM((packs, plane, LANES), jnp.float32),
            pltpu.VMEM((rim_slots, packs, plane, LANES), jnp.float32),
            pltpu.VMEM((4, tall, levels, width), jnp.float32),
            pltpu.VMEM((5, tall, levels, width), jnp.float32),
            pltpu.VMEM((fields * fields, levels, LANES), jnp.float32),
            pltpu.VMEM((SUBSTEPS + 1, fields, tall, levels, width), jnp.float32),
            pltpu.VMEM((rows, circle), jnp.float32),
            dma((2, DEPTH)), dma((2, DEPTH)), dma((2, DEPTH, peers - 1)), dma((2, DEPTH, peers - 1)),
            dma((5,)), dma((2,)), dma((2, peers - 1)), dma((2, peers - 1)),
            dma((2, rim_slots)), dma((2, rim_slots)),
            dma((3,)), dma((3,)), dma((rounds, 2)), dma((rounds, 2)),
        ],
        compiler_params=pltpu.CompilerParams(
            collective_id=0, has_side_effects=True, vmem_limit_bytes=VMEM_BYTES
        ),
    )(adjoint_in.reshape(fields, plane, sector), *flat, jnp.transpose(coupling, (1, 0, 2)), cutoff, jnp.asarray(forward), jnp.asarray(inverse))
    return out.reshape(fields, levels, rows, sector)


def solution(mesh):
    placed = (
        P("member", "lev", "lat", "lon"),
        P(("member", "lev"), "lat", "lon"),
        P(("member", "lev"), "lat", "lon"),
        P(("member", "lev"), "lat", "lon"),
        P(("member", "lev"), "lat", "lon"),
        P("lev", None, None),
        P(),
    )
    return jax.shard_map(
        functools.partial(shards, mesh.shape["lon"], mesh.shape["lat"]),
        mesh=mesh,
        in_specs=placed,
        out_specs=P("member", "lev", "lat", "lon"),
        check_vma=False,
    )
```

```python
import functools

import jax
import jax.numpy as jnp
import numpy as np
from jax import lax
from jax.experimental import pallas as pl
from jax.experimental.pallas import tpu as pltpu
from jax.sharding import PartitionSpec as P

SUBSTEPS = 6
ROUNDS = (4, 2)
DEPTH = ROUNDS[0]
STARTS = tuple(sum(ROUNDS[:r]) for r in range(len(ROUNDS)))
RIM = 16
LANES = 128
VMEM_BYTES = 66_200_000
MESH = pl.DeviceIdType.MESH


def split_parts(table):
    high = table.astype(jnp.bfloat16)
    low = (table - high.astype(np.float32)).astype(jnp.bfloat16)
    return np.stack([high, low])


def tables(circle, sector, width):
    column = np.arange(circle)
    middle = circle // 2
    wavenumber = np.where(column <= middle, column, column - middle)
    position = np.arange(circle)
    phase = (position[:, None] * wavenumber[None, :]) % circle
    angle = phase * (2.0 * np.pi / circle)
    weight = np.where((column == 0) | (column == middle), 1.0 / circle, 2.0 / circle)
    basis = np.where((column <= middle)[None, :], np.cos(angle), np.sin(angle))
    basis = (basis * np.sqrt(weight)[None, :]).astype(np.float32)
    lane = np.arange(width)
    target = np.where(lane < sector + RIM, lane, lane - width) % circle
    return split_parts(basis), split_parts(np.ascontiguousarray(basis[target].T))


def halves(values):
    high = values.astype(jnp.bfloat16)
    low = (values - high.astype(jnp.float32)).astype(jnp.bfloat16)
    return high, low


def product(values, high_table, low_table):
    high, low = halves(values)
    dot = functools.partial(jnp.dot, preferred_element_type=jnp.float32)
    return dot(high, high_table) + (dot(high, low_table) + dot(low, high_table))


def kernel(
    peers, bands, fields, rows, levels, sector, width,
    x_hbm, rates_hbm, couple_ref, cutoff_ref, forward_hbm, inverse_hbm, out_ref,
    raw, raw_rim, raw_swap, x_ref, rate_ref, forward, inverse, swapped, spectra, filtered, rate_rows, packed, rim, rates, coefs, power, state, damp_ref,
    raw_send, raw_recv, pass_send, pass_recv, load_sem, table_sem, swap_send, swap_recv, rim_send, rim_recv, rate_send, rate_recv, edge_send, edge_recv,
):
    chunks = 2
    lat = lax.axis_index("lat")
    lon = lax.axis_index("lon")
    quarter = bands // 4
    depth = DEPTH

    def in_polar(band):
        return (band < quarter) | (band >= 3 * quarter)

    polar = in_polar(lat)
    has_prev = lat > 0
    has_next = lat < bands - 1
    prev_polar = has_prev & in_polar(lat - 1)
    next_polar = has_next & in_polar(lat + 1)
    filters = polar | prev_polar | next_polar
    plane = rows * levels
    part = plane // chunks
    tail = sector % LANES
    body = sector - tail

    def lon_id(d):
        return {"lon": lax.rem(lon + d + peers, peers)}

    barrier = pltpu.get_barrier_semaphore()
    for d in range(1, peers):
        pl.semaphore_signal(barrier, inc=1, device_id=lon_id(d), device_id_type=MESH)

    @pl.when(has_prev)
    def _():
        pl.semaphore_signal(barrier, inc=1, device_id={"lat": lat - 1}, device_id_type=MESH)

    @pl.when(has_next)
    def _():
        pl.semaphore_signal(barrier, inc=1, device_id={"lat": lat + 1}, device_id_type=MESH)

    rate_refs = [rate_ref.at[r] for r in range(4)]
    loads = [pltpu.make_async_copy(x_hbm, x_ref, load_sem.at[4])]
    loads += [pltpu.make_async_copy(rates_hbm[r], rate_ref.at[r], load_sem.at[r]) for r in range(4)]
    for copy in loads:
        copy.start()

    table_copies = [
        pltpu.make_async_copy(forward_hbm, forward, table_sem.at[0]),
        pltpu.make_async_copy(inverse_hbm, inverse, table_sem.at[1]),
    ]

    @pl.when(filters)
    def _():
        for copy in table_copies:
            copy.start()

    greeters = peers - 1 + has_prev.astype(jnp.int32) + has_next.astype(jnp.int32)
    pl.semaphore_wait(barrier, greeters)

    swaps = [
        [
            pltpu.make_async_remote_copy(
                src_ref=x_hbm.at[:, pl.ds(c * part, part)],
                dst_ref=swapped.at[d - 1, :, pl.ds(c * part, part)],
                send_sem=swap_send.at[c, d - 1], recv_sem=swap_recv.at[c, d - 1],
                device_id=lon_id(-d), device_id_type=MESH,
            )
            for d in range(1, peers)
        ]
        for c in range(chunks)
    ]

    @pl.when(polar)
    def _():
        for copy in swaps[0]:
            copy.start()

    for copy in loads:
        copy.wait()

    def row_of(ref, j):
        return jnp.concatenate(
            [ref[t, pl.ds(j, levels, rows), :] for t in range(width // LANES)], axis=1
        )

    def raw_copy(side, row):
        source = rows - depth + row if side == 0 else row
        return pltpu.make_async_remote_copy(
            src_ref=raw.at[:, source], dst_ref=raw_rim.at[side, :, row],
            send_sem=raw_send.at[side, row], recv_sem=raw_recv.at[side, row],
            device_id={"lat": lat + 1 if side == 0 else lat - 1}, device_id_type=MESH,
        )

    def pass_copy(side, row, d):
        return pltpu.make_async_remote_copy(
            src_ref=raw_rim.at[side, :, row], dst_ref=raw_swap.at[side, d - 1, :, row],
            send_sem=pass_send.at[side, row, d - 1], recv_sem=pass_recv.at[side, row, d - 1],
            device_id=lon_id(-d), device_id_type=MESH,
        )

    @pl.when(polar)
    def _():
        for f in range(fields):
            for t in range(body // LANES):
                filtered[f, t] = x_ref[f, :, t * LANES:(t + 1) * LANES]
            filtered[f, body // LANES, :, 0:tail] = x_ref[f, :, body:sector]
            for j in sorted({*range(depth), *range(rows - depth, rows)}):
                raw[f, j] = row_of(filtered.at[f], j)[:, 0:sector]

        @pl.when(has_next)
        def _():
            for row in range(depth):
                raw_copy(0, row).start()

        @pl.when(has_prev)
        def _():
            for row in range(depth):
                raw_copy(1, row).start()

    sources = [r for r in rate_refs] + [x_ref.at[f] for f in range(fields)]
    lane = lax.broadcasted_iota(jnp.int32, (plane, LANES), 1)
    for block in range(packed.shape[0]):
        value = jnp.zeros((plane, LANES), jnp.float32)
        for k, source in enumerate(sources[4 * block:4 * block + 4]):
            first = source[:, 0:LANES]
            last = jnp.concatenate(
                [source[:, body:sector], jnp.zeros((plane, LANES - tail), jnp.float32)], axis=1
            )
            base = 32 * k
            if base:
                first = pltpu.roll(first, base, 1)
            last = pltpu.roll(last, (base + RIM - (tail - RIM)) % LANES, 1)
            value = jnp.where((lane >= base) & (lane < base + RIM), first, value)
            value = jnp.where((lane >= base + RIM) & (lane < base + 2 * RIM), last, value)
        packed[block] = value

    rim_slots = rim.shape[0]

    def rim_copies(stage, start, stop):
        return [
            pltpu.make_async_remote_copy(
                src_ref=packed.at[start:stop], dst_ref=rim.at[slot, start:stop],
                send_sem=rim_send.at[stage, slot], recv_sem=rim_recv.at[stage, slot],
                device_id=lon_id(-1 if slot == 0 else 1), device_id_type=MESH,
            )
            for slot in range(rim_slots)
        ]

    rate_rims, field_rims = rim_copies(0, 0, 1), rim_copies(1, 1, packed.shape[0])
    for copy in rate_rims:
        copy.start()

    @pl.when(polar)
    def _():
        for c in range(1, chunks):
            for copy in swaps[c]:
                copy.start()

    @pl.when(jnp.logical_not(polar))
    def _():
        for copy in field_rims:
            copy.start()

    def entry(g, f):
        value = jnp.broadcast_to(couple_ref[g, :, f:f + 1], (levels, LANES))
        return value + 1.0 if g == f else value

    once = [[entry(g, f) for f in range(fields)] for g in range(fields)]

    def multiply(a, b):
        return [
            [sum(a[g][h] * b[h][f] for h in range(fields)) for f in range(fields)]
            for g in range(fields)
        ]

    result = once
    for _ in range(SUBSTEPS - 1):
        result = multiply(result, once)
    for g in range(fields):
        for f in range(fields):
            power[g * fields + f] = result[g][f]

    @pl.when(jnp.logical_not(has_prev))
    def _():
        rates[:, 0:depth] = jnp.zeros((4, depth, levels, width), jnp.float32)
        for s in STARTS:
            state[s, :, 0:depth] = jnp.zeros((fields, depth, levels, width), jnp.float32)

    @pl.when(jnp.logical_not(has_next))
    def _():
        rates[:, depth + rows:] = jnp.zeros((4, depth, levels, width), jnp.float32)
        for s in STARTS:
            state[s, :, depth + rows:] = jnp.zeros((fields, depth, levels, width), jnp.float32)

    for copy in rate_rims:
        copy.wait()

    def with_rim(index, target):
        source = sources[index]
        block, base = index // 4, 32 * (index % 4)
        east = pltpu.roll(rim[0, block], (tail - base) % LANES, 1)
        west = pltpu.roll(rim[rim_slots - 1, block], (LANES - RIM - base - RIM) % LANES, 1)
        last = jnp.concatenate(
            [source[:, body:sector], jnp.zeros((plane, LANES - tail), jnp.float32)], axis=1
        )
        last = jnp.where((lane >= tail) & (lane < tail + RIM), east, last)
        last = jnp.where(lane >= LANES - RIM, west, last)
        for t in range(body // LANES):
            target[t] = source[:, t * LANES:(t + 1) * LANES]
        target[body // LANES] = last

    for r in range(4):
        with_rim(r, rate_rows.at[r])
    for r in range(4):
        for j in range(rows):
            rates[r, depth + j] = row_of(rate_rows.at[r], j)

    def to_neighbours(ref, reach, send, recv, prev_gives=True, self_gives=True, next_gives=True):
        to_prev = pltpu.make_async_remote_copy(
            src_ref=ref.at[:, pl.ds(depth, reach)], dst_ref=ref.at[:, pl.ds(depth + rows, reach)],
            send_sem=send.at[0], recv_sem=recv.at[0],
            device_id={"lat": lat - 1}, device_id_type=MESH,
        )
        to_next = pltpu.make_async_remote_copy(
            src_ref=ref.at[:, pl.ds(depth + rows - reach, reach)], dst_ref=ref.at[:, pl.ds(depth - reach, reach)],
            send_sem=send.at[1], recv_sem=recv.at[1],
            device_id={"lat": lat + 1}, device_id_type=MESH,
        )

        def start():
            pl.when(has_prev & self_gives)(to_prev.start)
            pl.when(has_next & self_gives)(to_next.start)

        def arrive():
            pl.when(has_next & next_gives)(to_prev.wait_recv)
            pl.when(has_prev & prev_gives)(to_next.wait_recv)

        def sent():
            pl.when(has_prev & self_gives)(to_prev.wait_send)
            pl.when(has_next & self_gives)(to_next.wait_send)

        return start, arrive, sent

    rate_start, rate_arrive, rate_sent = to_neighbours(rates, depth - 1, rate_send, rate_recv)
    behind = pltpu.make_async_remote_copy(
        src_ref=rates.at[1, rows], dst_ref=rates.at[1, 0],
        send_sem=rate_send.at[2], recv_sem=rate_recv.at[2],
        device_id={"lat": lat + 1}, device_id_type=MESH,
    )
    rate_start()
    pl.when(has_next)(behind.start)

    edges = []
    for r, reach in enumerate(ROUNDS):
        gives = (True, True, True)
        if r == 0:
            gives = tuple(jnp.logical_not(p) for p in (prev_polar, polar, next_polar))
        edges.append(to_neighbours(state.at[STARTS[r]], reach, edge_send.at[r], edge_recv.at[r], *gives))

    def mix(values, target):
        for f in range(fields):
            total = None
            for g in range(fields):
                term = jnp.tile(power[g * fields + f], (1, width // LANES)) * values[g]
                total = term if total is None else total + term
            state[0, f, target] = total

    def couple(j):
        mix([row_of(filtered.at[g], j) for g in range(fields)], depth + j)

    outer = sorted({*range(depth), *range(rows - depth, rows)})
    inner = [j for j in range(rows) if j not in outer]

    @pl.when(jnp.logical_not(polar))
    def _():
        for copy in field_rims:
            copy.wait()
        for f in range(fields):
            with_rim(4 + f, filtered.at[f])
        for j in outer:
            couple(j)
        edges[0][0]()
        for j in inner:
            couple(j)

    sides = ((0, prev_polar), (1, next_polar))
    for side, present in sides:
        @pl.when(present)
        def _():
            for row in range(depth):
                raw_copy(side, row).wait_recv()
                for d in range(1, peers):
                    pass_copy(side, row, d).start()

    modes = peers * sector

    def damping(shape, limit):
        column = lax.broadcasted_iota(jnp.int32, shape, 1)
        number = jnp.where(column <= modes // 2, column, column - modes // 2).astype(jnp.float32)
        ratio = limit / jnp.maximum(number, 1.0)
        return jnp.where(number > limit, ratio * ratio, 1.0)

    @pl.when(filters)
    def _():
        for copy in table_copies:
            copy.wait()

    @pl.when(polar)
    def _():
        row_index = lax.broadcasted_iota(jnp.int32, (rows, modes), 0)
        limit = jnp.zeros((rows, modes), jnp.float32)
        for j in range(rows):
            limit = jnp.where(row_index == j, cutoff_ref[lat * rows + j].astype(jnp.float32), limit)
        damp_ref[...] = damping((rows, modes), limit)
        for c in range(chunks):
            own = x_ref[:, c * part:(c + 1) * part].reshape(fields * part, sector)
            spectra[c] = product(own, forward[0, 0:sector], forward[1, 0:sector])

    rate_arrive()
    pl.when(has_prev)(behind.wait_recv)
    below_last = jnp.where(has_next, 1.0, 0.0)
    for j in range(1, rows + 2 * depth - 1):
        north = rates[0, j]
        if j == depth + rows - 1:
            north = north * below_last
        south = rates[1, j - 1]
        east = rates[2, j]
        west = pltpu.roll(rates[3, j], 1, 1)
        coefs[0, j] = 1.0 - east - west - north - south
        coefs[1, j] = east
        coefs[2, j] = west
        coefs[3, j] = north
        coefs[4, j] = south

    @pl.when(polar)
    def _():
        for c in range(chunks):
            for copy in swaps[c]:
                copy.wait_recv()
            total = spectra[c]
            for d in range(1, peers):
                values = swapped[d - 1, :, c * part:(c + 1) * part].reshape(fields * part, sector)
                start, end = d * sector, (d + 1) * sector
                total = total + product(values, forward[0, start:end], forward[1, start:end])
            damped = total.reshape(fields * part // rows, rows, modes) * damp_ref[...][None]
            result = product(damped.reshape(fields * part, modes), inverse[0], inverse[1])
            for t in range(width // LANES):
                block = result[:, t * LANES:(t + 1) * LANES].reshape(fields, part, LANES)
                filtered[:, t, c * part:(c + 1) * part] = block
        for j in range(rows):
            couple(j)

    for side, present in sides:
        @pl.when(present)
        def _():
            count = fields * depth * levels
            total = product(raw_rim[side].reshape(count, sector), forward[0, 0:sector], forward[1, 0:sector])
            for d in range(1, peers):
                for row in range(depth):
                    pass_copy(side, row, d).wait_recv()
                start, end = d * sector, (d + 1) * sector
                total = total + product(
                    raw_swap[side, d - 1].reshape(count, sector), forward[0, start:end], forward[1, start:end]
                )
            begin = lat * rows - depth if side == 0 else (lat + 1) * rows
            limits = [cutoff_ref[begin + row].astype(jnp.float32) for row in range(depth)]
            table = jnp.stack([damping((levels, modes), limit) for limit in limits])
            damped = total.reshape(fields, depth, levels, modes) * table[None]
            result = product(damped.reshape(count, modes), inverse[0], inverse[1])
            result = result.reshape(fields, depth, levels, width)
            for row in range(depth):
                mix([result[g, row] for g in range(fields)], row if side == 0 else depth + rows + row)

    def advance(s, j):
        rate = [coefs[k, j] for k in range(5)]
        for f in range(fields):
            here = state[s, f, j]
            value = (
                rate[0] * here
                + rate[1] * pltpu.roll(here, width - 1, 1)
                + rate[2] * pltpu.roll(here, 1, 1)
                + rate[3] * state[s, f, j + 1]
                + rate[4] * state[s, f, j - 1]
            )
            state[s + 1, f, j] = value

    def advance_rows(s, start, end):
        if end > start:
            @pl.loop(start, end, step=2)
            def _(j):
                advance(s, j)
                advance(s, j + 1)

    for r, first in enumerate(STARTS):
        edges[r][1]()
        for k in range(ROUNDS[r]):
            s = first + k
            reach = ROUNDS[r] - 1 - k
            if reach == 0 and s + 1 < SUBSTEPS:
                ahead = ROUNDS[r + 1]
                advance_rows(s, depth, depth + ahead)
                advance_rows(s, depth + rows - ahead, depth + rows)
                edges[r + 1][0]()
                advance_rows(s, depth + ahead, depth + rows - ahead)
            else:
                advance_rows(s, depth - reach, depth + rows + reach)

    for f in range(fields):
        for j in range(rows):
            value = state[SUBSTEPS, f, depth + j]
            for t in range(width // LANES):
                filtered[f, t, pl.ds(j, levels, rows), :] = value[:, t * LANES:(t + 1) * LANES]
    for t in range(width // LANES):
        end = min(sector, (t + 1) * LANES)
        out_ref[:, :, t * LANES:end] = filtered[:, t, :, 0:end - t * LANES]

    rate_sent()
    pl.when(has_next)(behind.wait_send)
    for edge in edges:
        edge[2]()

    @pl.when(polar)
    def _():
        for c in range(chunks):
            for copy in swaps[c]:
                copy.wait_send()

        @pl.when(has_next)
        def _():
            for row in range(depth):
                raw_copy(0, row).wait_send()

        @pl.when(has_prev)
        def _():
            for row in range(depth):
                raw_copy(1, row).wait_send()

    for side, present in sides:
        @pl.when(present)
        def _():
            for row in range(depth):
                for d in range(1, peers):
                    pass_copy(side, row, d).wait_send()


def shards(peers, bands, adjoint_in, lat_ahead, lat_behind, lon_ahead, lon_behind, coupling, cutoff):
    fields, levels, rows, sector = adjoint_in.shape
    width = -(-(sector + 2 * RIM) // LANES) * LANES
    circle = sector * peers
    forward, inverse = tables(circle, sector, width)
    plane = rows * levels
    flat = [r.reshape(plane, sector) for r in (lat_ahead, lat_behind, lon_ahead, lon_behind)]
    vmem = pl.BlockSpec(memory_space=pltpu.VMEM)
    hbm = pl.BlockSpec(memory_space=pltpu.HBM)
    smem = pl.BlockSpec(memory_space=pltpu.SMEM)
    rim_slots = 1 if peers == 2 else 2
    packs = -(-(4 + fields) // 4)
    tall = rows + 2 * DEPTH
    rounds = len(ROUNDS)

    def body(x, a, b, c, d, *rest):
        kernel(peers, bands, fields, rows, levels, sector, width, x, [a, b, c, d], *rest)

    dma = pltpu.SemaphoreType.DMA
    out = pl.pallas_call(
        body,
        out_shape=pltpu.VMEM((fields, plane, sector), jnp.float32),
        in_specs=[hbm] * 5 + [vmem, smem] + [hbm] * 2,
        out_specs=vmem,
        scratch_shapes=[
            pltpu.VMEM((fields, rows, levels, sector), jnp.float32),
            pltpu.VMEM((2, fields, DEPTH, levels, sector), jnp.float32),
            pltpu.VMEM((2, peers - 1, fields, DEPTH, levels, sector), jnp.float32),
            pltpu.VMEM((fields, plane, sector), jnp.float32),
            pltpu.VMEM((4, plane, sector), jnp.float32),
            pltpu.VMEM(forward.shape, jnp.bfloat16),
            pltpu.VMEM(inverse.shape, jnp.bfloat16),
            pltpu.VMEM((peers - 1, fields, plane, sector), jnp.float32),
            pltpu.VMEM((2, fields * plane // 2, circle), jnp.float32),
            pltpu.VMEM((fields, width // LANES, plane, LANES), jnp.float32),
            pltpu.VMEM((4, width // LANES, plane, LANES), jnp.float32),
            pltpu.VMEM((packs, plane, LANES), jnp.float32),
            pltpu.VMEM((rim_slots, packs, plane, LANES), jnp.float32),
            pltpu.VMEM((4, tall, levels, width), jnp.float32),
            pltpu.VMEM((5, tall, levels, width), jnp.float32),
            pltpu.VMEM((fields * fields, levels, LANES), jnp.float32),
            pltpu.VMEM((SUBSTEPS + 1, fields, tall, levels, width), jnp.float32),
            pltpu.VMEM((rows, circle), jnp.float32),
            dma((2, DEPTH)), dma((2, DEPTH)), dma((2, DEPTH, peers - 1)), dma((2, DEPTH, peers - 1)),
            dma((5,)), dma((2,)), dma((2, peers - 1)), dma((2, peers - 1)),
            dma((2, rim_slots)), dma((2, rim_slots)),
            dma((3,)), dma((3,)), dma((rounds, 2)), dma((rounds, 2)),
        ],
        compiler_params=pltpu.CompilerParams(
            collective_id=0, has_side_effects=True, vmem_limit_bytes=VMEM_BYTES
        ),
    )(adjoint_in.reshape(fields, plane, sector), *flat, jnp.transpose(coupling, (1, 0, 2)), cutoff, jnp.asarray(forward), jnp.asarray(inverse))
    return out.reshape(fields, levels, rows, sector)


def solution(mesh):
    placed = (
        P("member", "lev", "lat", "lon"),
        P(("member", "lev"), "lat", "lon"),
        P(("member", "lev"), "lat", "lon"),
        P(("member", "lev"), "lat", "lon"),
        P(("member", "lev"), "lat", "lon"),
        P("lev", None, None),
        P(),
    )
    return jax.shard_map(
        functools.partial(shards, mesh.shape["lon"], mesh.shape["lat"]),
        mesh=mesh,
        in_specs=placed,
        out_specs=P("member", "lev", "lat", "lon"),
        check_vma=False,
    )
```

```python
import functools

import jax
import jax.numpy as jnp
import numpy as np
from jax import lax
from jax.experimental import pallas as pl
from jax.experimental.pallas import tpu as pltpu
from jax.sharding import PartitionSpec as P

SUBSTEPS = 6
ROUNDS = (5, 1)
DEPTH = ROUNDS[0]
STARTS = tuple(sum(ROUNDS[:r]) for r in range(len(ROUNDS)))
RIM = 16
LANES = 128
VMEM_BYTES = 66_200_000
MESH = pl.DeviceIdType.MESH


def split_parts(table):
    high = table.astype(jnp.bfloat16)
    low = (table - high.astype(np.float32)).astype(jnp.bfloat16)
    return np.stack([high, low])


def tables(circle, sector, width):
    column = np.arange(circle)
    middle = circle // 2
    wavenumber = np.where(column <= middle, column, column - middle)
    position = np.arange(circle)
    phase = (position[:, None] * wavenumber[None, :]) % circle
    angle = phase * (2.0 * np.pi / circle)
    weight = np.where((column == 0) | (column == middle), 1.0 / circle, 2.0 / circle)
    basis = np.where((column <= middle)[None, :], np.cos(angle), np.sin(angle))
    basis = (basis * np.sqrt(weight)[None, :]).astype(np.float32)
    lane = np.arange(width)
    target = np.where(lane < sector + RIM, lane, lane - width) % circle
    return split_parts(basis), split_parts(np.ascontiguousarray(basis[target].T))


def halves(values):
    high = values.astype(jnp.bfloat16)
    low = (values - high.astype(jnp.float32)).astype(jnp.bfloat16)
    return high, low


def product(values, high_table, low_table):
    high, low = halves(values)
    dot = functools.partial(jnp.dot, preferred_element_type=jnp.float32)
    return dot(high, high_table) + (dot(high, low_table) + dot(low, high_table))


def kernel(
    peers, bands, fields, rows, levels, sector, width,
    x_hbm, rates_hbm, couple_ref, cutoff_ref, forward_hbm, inverse_hbm, out_ref,
    raw, raw_rim, raw_swap, x_ref, rate_ref, forward, inverse, swapped, spectra, filtered, rate_rows, packed, rim, rates, coefs, power, state, damp_ref,
    raw_send, raw_recv, pass_send, pass_recv, load_sem, table_sem, swap_send, swap_recv, rim_send, rim_recv, rate_send, rate_recv, edge_send, edge_recv,
):
    chunks = 2
    lat = lax.axis_index("lat")
    lon = lax.axis_index("lon")
    quarter = bands // 4
    depth = DEPTH

    def in_polar(band):
        return (band < quarter) | (band >= 3 * quarter)

    polar = in_polar(lat)
    has_prev = lat > 0
    has_next = lat < bands - 1
    prev_polar = has_prev & in_polar(lat - 1)
    next_polar = has_next & in_polar(lat + 1)
    filters = polar | prev_polar | next_polar
    plane = rows * levels
    part = plane // chunks
    tail = sector % LANES
    body = sector - tail

    def lon_id(d):
        return {"lon": lax.rem(lon + d + peers, peers)}

    barrier = pltpu.get_barrier_semaphore()
    for d in range(1, peers):
        pl.semaphore_signal(barrier, inc=1, device_id=lon_id(d), device_id_type=MESH)

    @pl.when(has_prev)
    def _():
        pl.semaphore_signal(barrier, inc=1, device_id={"lat": lat - 1}, device_id_type=MESH)

    @pl.when(has_next)
    def _():
        pl.semaphore_signal(barrier, inc=1, device_id={"lat": lat + 1}, device_id_type=MESH)

    rate_refs = [rate_ref.at[r] for r in range(4)]
    loads = [pltpu.make_async_copy(x_hbm, x_ref, load_sem.at[4])]
    loads += [pltpu.make_async_copy(rates_hbm[r], rate_ref.at[r], load_sem.at[r]) for r in range(4)]
    for copy in loads:
        copy.start()

    table_copies = [
        pltpu.make_async_copy(forward_hbm, forward, table_sem.at[0]),
        pltpu.make_async_copy(inverse_hbm, inverse, table_sem.at[1]),
    ]

    @pl.when(filters)
    def _():
        for copy in table_copies:
            copy.start()

    greeters = peers - 1 + has_prev.astype(jnp.int32) + has_next.astype(jnp.int32)
    pl.semaphore_wait(barrier, greeters)

    swaps = [
        [
            pltpu.make_async_remote_copy(
                src_ref=x_hbm.at[:, pl.ds(c * part, part)],
                dst_ref=swapped.at[d - 1, :, pl.ds(c * part, part)],
                send_sem=swap_send.at[c, d - 1], recv_sem=swap_recv.at[c, d - 1],
                device_id=lon_id(-d), device_id_type=MESH,
            )
            for d in range(1, peers)
        ]
        for c in range(chunks)
    ]

    @pl.when(polar)
    def _():
        for copy in swaps[0]:
            copy.start()

    for copy in loads:
        copy.wait()

    def row_of(ref, j):
        return jnp.concatenate(
            [ref[t, pl.ds(j, levels, rows), :] for t in range(width // LANES)], axis=1
        )

    def raw_copy(side, row):
        source = rows - depth + row if side == 0 else row
        return pltpu.make_async_remote_copy(
            src_ref=raw.at[:, source], dst_ref=raw_rim.at[side, :, row],
            send_sem=raw_send.at[side, row], recv_sem=raw_recv.at[side, row],
            device_id={"lat": lat + 1 if side == 0 else lat - 1}, device_id_type=MESH,
        )

    def pass_copy(side, row, d):
        return pltpu.make_async_remote_copy(
            src_ref=raw_rim.at[side, :, row], dst_ref=raw_swap.at[side, d - 1, :, row],
            send_sem=pass_send.at[side, row, d - 1], recv_sem=pass_recv.at[side, row, d - 1],
            device_id=lon_id(-d), device_id_type=MESH,
        )

    @pl.when(polar)
    def _():
        for f in range(fields):
            for t in range(body // LANES):
                filtered[f, t] = x_ref[f, :, t * LANES:(t + 1) * LANES]
            filtered[f, body // LANES, :, 0:tail] = x_ref[f, :, body:sector]
            for j in sorted({*range(depth), *range(rows - depth, rows)}):
                raw[f, j] = row_of(filtered.at[f], j)[:, 0:sector]

        @pl.when(has_next)
        def _():
            for row in range(depth):
                raw_copy(0, row).start()

        @pl.when(has_prev)
        def _():
            for row in range(depth):
                raw_copy(1, row).start()

    sources = [r for r in rate_refs] + [x_ref.at[f] for f in range(fields)]
    lane = lax.broadcasted_iota(jnp.int32, (plane, LANES), 1)
    for block in range(packed.shape[0]):
        value = jnp.zeros((plane, LANES), jnp.float32)
        for k, source in enumerate(sources[4 * block:4 * block + 4]):
            first = source[:, 0:LANES]
            last = jnp.concatenate(
                [source[:, body:sector], jnp.zeros((plane, LANES - tail), jnp.float32)], axis=1
            )
            base = 32 * k
            if base:
                first = pltpu.roll(first, base, 1)
            last = pltpu.roll(last, (base + RIM - (tail - RIM)) % LANES, 1)
            value = jnp.where((lane >= base) & (lane < base + RIM), first, value)
            value = jnp.where((lane >= base + RIM) & (lane < base + 2 * RIM), last, value)
        packed[block] = value

    rim_slots = rim.shape[0]

    def rim_copies(stage, start, stop):
        return [
            pltpu.make_async_remote_copy(
                src_ref=packed.at[start:stop], dst_ref=rim.at[slot, start:stop],
                send_sem=rim_send.at[stage, slot], recv_sem=rim_recv.at[stage, slot],
                device_id=lon_id(-1 if slot == 0 else 1), device_id_type=MESH,
            )
            for slot in range(rim_slots)
        ]

    rate_rims, field_rims = rim_copies(0, 0, 1), rim_copies(1, 1, packed.shape[0])
    for copy in rate_rims:
        copy.start()

    @pl.when(polar)
    def _():
        for c in range(1, chunks):
            for copy in swaps[c]:
                copy.start()

    @pl.when(jnp.logical_not(polar))
    def _():
        for copy in field_rims:
            copy.start()

    def entry(g, f):
        value = jnp.broadcast_to(couple_ref[g, :, f:f + 1], (levels, LANES))
        return value + 1.0 if g == f else value

    once = [[entry(g, f) for f in range(fields)] for g in range(fields)]

    def multiply(a, b):
        return [
            [sum(a[g][h] * b[h][f] for h in range(fields)) for f in range(fields)]
            for g in range(fields)
        ]

    result = once
    for _ in range(SUBSTEPS - 1):
        result = multiply(result, once)
    for g in range(fields):
        for f in range(fields):
            power[g * fields + f] = result[g][f]

    @pl.when(jnp.logical_not(has_prev))
    def _():
        rates[:, 0:depth] = jnp.zeros((4, depth, levels, width), jnp.float32)
        for s in STARTS:
            state[s, :, 0:depth] = jnp.zeros((fields, depth, levels, width), jnp.float32)

    @pl.when(jnp.logical_not(has_next))
    def _():
        rates[:, depth + rows:] = jnp.zeros((4, depth, levels, width), jnp.float32)
        for s in STARTS:
            state[s, :, depth + rows:] = jnp.zeros((fields, depth, levels, width), jnp.float32)

    for copy in rate_rims:
        copy.wait()

    def with_rim(index, target):
        source = sources[index]
        block, base = index // 4, 32 * (index % 4)
        east = pltpu.roll(rim[0, block], (tail - base) % LANES, 1)
        west = pltpu.roll(rim[rim_slots - 1, block], (LANES - RIM - base - RIM) % LANES, 1)
        last = jnp.concatenate(
            [source[:, body:sector], jnp.zeros((plane, LANES - tail), jnp.float32)], axis=1
        )
        last = jnp.where((lane >= tail) & (lane < tail + RIM), east, last)
        last = jnp.where(lane >= LANES - RIM, west, last)
        for t in range(body // LANES):
            target[t] = source[:, t * LANES:(t + 1) * LANES]
        target[body // LANES] = last

    for r in range(4):
        with_rim(r, rate_rows.at[r])
    for r in range(4):
        for j in range(rows):
            rates[r, depth + j] = row_of(rate_rows.at[r], j)

    def to_neighbours(ref, reach, send, recv, prev_gives=True, self_gives=True, next_gives=True):
        to_prev = pltpu.make_async_remote_copy(
            src_ref=ref.at[:, pl.ds(depth, reach)], dst_ref=ref.at[:, pl.ds(depth + rows, reach)],
            send_sem=send.at[0], recv_sem=recv.at[0],
            device_id={"lat": lat - 1}, device_id_type=MESH,
        )
        to_next = pltpu.make_async_remote_copy(
            src_ref=ref.at[:, pl.ds(depth + rows - reach, reach)], dst_ref=ref.at[:, pl.ds(depth - reach, reach)],
            send_sem=send.at[1], recv_sem=recv.at[1],
            device_id={"lat": lat + 1}, device_id_type=MESH,
        )

        def start():
            pl.when(has_prev & self_gives)(to_prev.start)
            pl.when(has_next & self_gives)(to_next.start)

        def arrive():
            pl.when(has_next & next_gives)(to_prev.wait_recv)
            pl.when(has_prev & prev_gives)(to_next.wait_recv)

        def sent():
            pl.when(has_prev & self_gives)(to_prev.wait_send)
            pl.when(has_next & self_gives)(to_next.wait_send)

        return start, arrive, sent

    rate_start, rate_arrive, rate_sent = to_neighbours(rates, depth - 1, rate_send, rate_recv)
    behind = pltpu.make_async_remote_copy(
        src_ref=rates.at[1, rows], dst_ref=rates.at[1, 0],
        send_sem=rate_send.at[2], recv_sem=rate_recv.at[2],
        device_id={"lat": lat + 1}, device_id_type=MESH,
    )
    rate_start()
    pl.when(has_next)(behind.start)

    edges = []
    for r, reach in enumerate(ROUNDS):
        gives = (True, True, True)
        if r == 0:
            gives = tuple(jnp.logical_not(p) for p in (prev_polar, polar, next_polar))
        edges.append(to_neighbours(state.at[STARTS[r]], reach, edge_send.at[r], edge_recv.at[r], *gives))

    def mix(values, target):
        for f in range(fields):
            total = None
            for g in range(fields):
                term = jnp.tile(power[g * fields + f], (1, width // LANES)) * values[g]
                total = term if total is None else total + term
            state[0, f, target] = total

    def couple(j):
        mix([row_of(filtered.at[g], j) for g in range(fields)], depth + j)

    outer = sorted({*range(depth), *range(rows - depth, rows)})
    inner = [j for j in range(rows) if j not in outer]

    @pl.when(jnp.logical_not(polar))
    def _():
        for copy in field_rims:
            copy.wait()
        for f in range(fields):
            with_rim(4 + f, filtered.at[f])
        for j in outer:
            couple(j)
        edges[0][0]()
        for j in inner:
            couple(j)

    sides = ((0, prev_polar), (1, next_polar))
    for side, present in sides:
        @pl.when(present)
        def _():
            for row in range(depth):
                raw_copy(side, row).wait_recv()
                for d in range(1, peers):
                    pass_copy(side, row, d).start()

    modes = peers * sector

    def damping(shape, limit):
        column = lax.broadcasted_iota(jnp.int32, shape, 1)
        number = jnp.where(column <= modes // 2, column, column - modes // 2).astype(jnp.float32)
        ratio = limit / jnp.maximum(number, 1.0)
        return jnp.where(number > limit, ratio * ratio, 1.0)

    @pl.when(filters)
    def _():
        for copy in table_copies:
            copy.wait()

    @pl.when(polar)
    def _():
        row_index = lax.broadcasted_iota(jnp.int32, (rows, modes), 0)
        limit = jnp.zeros((rows, modes), jnp.float32)
        for j in range(rows):
            limit = jnp.where(row_index == j, cutoff_ref[lat * rows + j].astype(jnp.float32), limit)
        damp_ref[...] = damping((rows, modes), limit)
        for c in range(chunks):
            own = x_ref[:, c * part:(c + 1) * part].reshape(fields * part, sector)
            spectra[c] = product(own, forward[0, 0:sector], forward[1, 0:sector])

    rate_arrive()
    pl.when(has_prev)(behind.wait_recv)
    below_last = jnp.where(has_next, 1.0, 0.0)
    for j in range(1, rows + 2 * depth - 1):
        north = rates[0, j]
        if j == depth + rows - 1:
            north = north * below_last
        south = rates[1, j - 1]
        east = rates[2, j]
        west = pltpu.roll(rates[3, j], 1, 1)
        coefs[0, j] = 1.0 - east - west - north - south
        coefs[1, j] = east
        coefs[2, j] = west
        coefs[3, j] = north
        coefs[4, j] = south

    @pl.when(polar)
    def _():
        for c in range(chunks):
            for copy in swaps[c]:
                copy.wait_recv()
            total = spectra[c]
            for d in range(1, peers):
                values = swapped[d - 1, :, c * part:(c + 1) * part].reshape(fields * part, sector)
                start, end = d * sector, (d + 1) * sector
                total = total + product(values, forward[0, start:end], forward[1, start:end])
            damped = total.reshape(fields * part // rows, rows, modes) * damp_ref[...][None]
            result = product(damped.reshape(fields * part, modes), inverse[0], inverse[1])
            for t in range(width // LANES):
                block = result[:, t * LANES:(t + 1) * LANES].reshape(fields, part, LANES)
                filtered[:, t, c * part:(c + 1) * part] = block
        for j in range(rows):
            couple(j)

    for side, present in sides:
        @pl.when(present)
        def _():
            count = fields * depth * levels
            total = product(raw_rim[side].reshape(count, sector), forward[0, 0:sector], forward[1, 0:sector])
            for d in range(1, peers):
                for row in range(depth):
                    pass_copy(side, row, d).wait_recv()
                start, end = d * sector, (d + 1) * sector
                total = total + product(
                    raw_swap[side, d - 1].reshape(count, sector), forward[0, start:end], forward[1, start:end]
                )
            begin = lat * rows - depth if side == 0 else (lat + 1) * rows
            limits = [cutoff_ref[begin + row].astype(jnp.float32) for row in range(depth)]
            table = jnp.stack([damping((levels, modes), limit) for limit in limits])
            damped = total.reshape(fields, depth, levels, modes) * table[None]
            result = product(damped.reshape(count, modes), inverse[0], inverse[1])
            result = result.reshape(fields, depth, levels, width)
            for row in range(depth):
                mix([result[g, row] for g in range(fields)], row if side == 0 else depth + rows + row)

    def advance(s, j):
        rate = [coefs[k, j] for k in range(5)]
        for f in range(fields):
            here = state[s, f, j]
            value = (
                rate[0] * here
                + rate[1] * pltpu.roll(here, width - 1, 1)
                + rate[2] * pltpu.roll(here, 1, 1)
                + rate[3] * state[s, f, j + 1]
                + rate[4] * state[s, f, j - 1]
            )
            state[s + 1, f, j] = value

    def advance_rows(s, start, end):
        half = (end - start) // 2
        if half < 2 or (end - start) % 2:
            for j in range(start, end):
                advance(s, j)
        else:
            @pl.loop(start, end, step=half)
            def _(j):
                for offset in range(half):
                    advance(s, j + offset)

    for r, first in enumerate(STARTS):
        edges[r][1]()
        for k in range(ROUNDS[r]):
            s = first + k
            reach = ROUNDS[r] - 1 - k
            if reach == 0 and s + 1 < SUBSTEPS:
                ahead = ROUNDS[r + 1]
                advance_rows(s, depth, depth + ahead)
                advance_rows(s, depth + rows - ahead, depth + rows)
                edges[r + 1][0]()
                advance_rows(s, depth + ahead, depth + rows - ahead)
            else:
                advance_rows(s, depth - reach, depth + rows + reach)

    for f in range(fields):
        for j in range(rows):
            value = state[SUBSTEPS, f, depth + j]
            for t in range(width // LANES):
                filtered[f, t, pl.ds(j, levels, rows), :] = value[:, t * LANES:(t + 1) * LANES]
    for t in range(width // LANES):
        end = min(sector, (t + 1) * LANES)
        out_ref[:, :, t * LANES:end] = filtered[:, t, :, 0:end - t * LANES]

    rate_sent()
    pl.when(has_next)(behind.wait_send)
    for edge in edges:
        edge[2]()

    @pl.when(polar)
    def _():
        for c in range(chunks):
            for copy in swaps[c]:
                copy.wait_send()

        @pl.when(has_next)
        def _():
            for row in range(depth):
                raw_copy(0, row).wait_send()

        @pl.when(has_prev)
        def _():
            for row in range(depth):
                raw_copy(1, row).wait_send()

    for side, present in sides:
        @pl.when(present)
        def _():
            for row in range(depth):
                for d in range(1, peers):
                    pass_copy(side, row, d).wait_send()


def shards(peers, bands, adjoint_in, lat_ahead, lat_behind, lon_ahead, lon_behind, coupling, cutoff):
    fields, levels, rows, sector = adjoint_in.shape
    width = -(-(sector + 2 * RIM) // LANES) * LANES
    circle = sector * peers
    forward, inverse = tables(circle, sector, width)
    plane = rows * levels
    flat = [r.reshape(plane, sector) for r in (lat_ahead, lat_behind, lon_ahead, lon_behind)]
    vmem = pl.BlockSpec(memory_space=pltpu.VMEM)
    hbm = pl.BlockSpec(memory_space=pltpu.HBM)
    smem = pl.BlockSpec(memory_space=pltpu.SMEM)
    rim_slots = 1 if peers == 2 else 2
    packs = -(-(4 + fields) // 4)
    tall = rows + 2 * DEPTH
    rounds = len(ROUNDS)

    def body(x, a, b, c, d, *rest):
        kernel(peers, bands, fields, rows, levels, sector, width, x, [a, b, c, d], *rest)

    dma = pltpu.SemaphoreType.DMA
    out = pl.pallas_call(
        body,
        out_shape=pltpu.VMEM((fields, plane, sector), jnp.float32),
        in_specs=[hbm] * 5 + [vmem, smem] + [hbm] * 2,
        out_specs=vmem,
        scratch_shapes=[
            pltpu.VMEM((fields, rows, levels, sector), jnp.float32),
            pltpu.VMEM((2, fields, DEPTH, levels, sector), jnp.float32),
            pltpu.VMEM((2, peers - 1, fields, DEPTH, levels, sector), jnp.float32),
            pltpu.VMEM((fields, plane, sector), jnp.float32),
            pltpu.VMEM((4, plane, sector), jnp.float32),
            pltpu.VMEM(forward.shape, jnp.bfloat16),
            pltpu.VMEM(inverse.shape, jnp.bfloat16),
            pltpu.VMEM((peers - 1, fields, plane, sector), jnp.float32),
            pltpu.VMEM((2, fields * plane // 2, circle), jnp.float32),
            pltpu.VMEM((fields, width // LANES, plane, LANES), jnp.float32),
            pltpu.VMEM((4, width // LANES, plane, LANES), jnp.float32),
            pltpu.VMEM((packs, plane, LANES), jnp.float32),
            pltpu.VMEM((rim_slots, packs, plane, LANES), jnp.float32),
            pltpu.VMEM((4, tall, levels, width), jnp.float32),
            pltpu.VMEM((5, tall, levels, width), jnp.float32),
            pltpu.VMEM((fields * fields, levels, LANES), jnp.float32),
            pltpu.VMEM((SUBSTEPS + 1, fields, tall, levels, width), jnp.float32),
            pltpu.VMEM((rows, circle), jnp.float32),
            dma((2, DEPTH)), dma((2, DEPTH)), dma((2, DEPTH, peers - 1)), dma((2, DEPTH, peers - 1)),
            dma((5,)), dma((2,)), dma((2, peers - 1)), dma((2, peers - 1)),
            dma((2, rim_slots)), dma((2, rim_slots)),
            dma((3,)), dma((3,)), dma((rounds, 2)), dma((rounds, 2)),
        ],
        compiler_params=pltpu.CompilerParams(
            collective_id=0, has_side_effects=True, vmem_limit_bytes=VMEM_BYTES
        ),
    )(adjoint_in.reshape(fields, plane, sector), *flat, jnp.transpose(coupling, (1, 0, 2)), cutoff, jnp.asarray(forward), jnp.asarray(inverse))
    return out.reshape(fields, levels, rows, sector)


def solution(mesh):
    placed = (
        P("member", "lev", "lat", "lon"),
        P(("member", "lev"), "lat", "lon"),
        P(("member", "lev"), "lat", "lon"),
        P(("member", "lev"), "lat", "lon"),
        P(("member", "lev"), "lat", "lon"),
        P("lev", None, None),
        P(),
    )
    return jax.shard_map(
        functools.partial(shards, mesh.shape["lon"], mesh.shape["lat"]),
        mesh=mesh,
        in_specs=placed,
        out_specs=P("member", "lev", "lat", "lon"),
        check_vma=False,
    )
```
